256 devices in a mesh: lat: 16 (over y, x_hi, core), lon: 16 (over z, x_lo).
Axes of the slice: x: 4 (x_hi: 2, x_lo: 2; x = x_hi * 2 + x_lo), y: 4, z: 8, core: 2. Of those that a mesh axis runs over, the one named last changes fastest.
Arguments:
- tracers: float32 [2, 8, 2432, 4096], P(None, None, 'lat', 'lon'), may hold values from -6 to 6
- east_faces: float32 [2, 8, 2432, 4096], P(None, None, 'lat', 'lon'), may hold values from -0.5 to 0.5, as said below
- north_faces: float32 [2, 8, 2432, 4096], P(None, None, 'lat', 'lon'), may hold values from -0.5 to 0.5, as said below
- land_mask: int32 [8, 2432, 4096], P(None, 'lat', 'lon'), may hold values from 0 to 1, as said below
- fold_partner: int32 [4096], P('lon'), may hold values from 0 to 4095, as said below
- vert_mix: float32 [7], replicated, may hold values from 0.05 to 0.3
Outputs:
- tracers_out: float32 [2, 8, 2432, 4096], P(None, None, 'lat', 'lon')
- density: float32 [8, 2432, 4096], P(None, 'lat', 'lon')
The draws below stay inside these ranges and needn't reach their ends.
Inputs may be any that keep to these rules, and one draw needn't show every extreme that they name: `land_mask`: A column is sea from the top level down to some depth and land below it; whole columns may be land. `fold_partner`: the partner of column i lies in the longitude tile of number (tiles along longitude) - 1 - (i // 256); the partners of one tile's columns are all distinct. `east_faces`: index 1 lies between 0 and 0.06. Both components are zero on every face with land on either side; the east face of the last column joins it to column 0, and the faces stand on sea cells only. `north_faces`: index 1 lies between 0 and 0.06. Both components are zero on every face with land on either side; the north face of the top row joins a cell to the top-row cell at its fold partner.
All inputs are finite; a program needn't handle non-finite values.
Results may differ from the reference program's by a relative error of at most 0.0003.
Values sent between devices are 32-bit elements; how exact they have to be, the bound alone decides.
No kernel may reach another device: no remote copies, remote signals or barrier semaphores. Data moves between devices by JAX's collectives and lax.ppermute only.
A program may use at most 128 MiB of HBM per device.

```python
import math
import jax
import jax.numpy as jnp
from jax import lax

CLAT = 152
CLON = 256
LEV = 8
STEPS = 2
NLAT = 2432
NLON = 4096
N_LON = 16


def sea_grid(key):
    column_depth = jax.random.randint(jax.random.fold_in(key, 7001), (NLAT, NLON), -1, 6 * LEV)
    level_grid = lax.broadcasted_iota(jnp.int32, (LEV, NLAT, NLON), 0)
    return (level_grid < column_depth[None]).astype(jnp.int32)


def partner_grid(key):
    tile_keys = jax.random.split(jax.random.fold_in(key, 7002), N_LON)
    shuffles = jax.vmap(lambda one_key: jax.random.permutation(one_key, CLON))(tile_keys).astype(jnp.int32)
    tile_index = lax.broadcasted_iota(jnp.int32, (N_LON, CLON), 0)
    return ((N_LON - 1 - tile_index) * CLON + shuffles).reshape(NLON)


def face_numbers(key, salt_value, open_faces, pinned):
    flow_key = jax.random.fold_in(key, salt_value)
    spread_key = jax.random.fold_in(key, salt_value + 1)
    strong_key = jax.random.fold_in(key, salt_value + 2)
    shape = (LEV, NLAT, NLON)
    strong = jax.random.uniform(strong_key, shape, jnp.float32, 0.45, 0.5)
    flow_number = jnp.clip(0.1 * jax.random.normal(flow_key, shape, jnp.float32), -0.3, 0.3)
    spread_number = jnp.exp(jax.random.uniform(spread_key, shape, jnp.float32, jnp.log(0.01), jnp.log(0.06)))
    flow_number = jnp.where(pinned != 0.0, pinned * strong, flow_number)
    return jnp.stack([flow_number * open_faces, spread_number * open_faces], axis=0)


def draw_tracers(key, part):
    key = jax.random.fold_in(key, 7011)
    shape = (2, LEV, NLAT, NLON)
    row_place = lax.broadcasted_iota(jnp.int32, shape, 2) % CLAT
    col_place = lax.broadcasted_iota(jnp.int32, shape, 3) % CLON
    ridge = (row_place == CLAT - 4) | (col_place == CLON - 4)
    line_draw = jax.random.uniform(jax.random.fold_in(key, 1), shape, jnp.float32, -1.0, 1.0)
    lines = jnp.where(line_draw >= 0.0, 3.0 + 3.0 * line_draw, -3.0 + 3.0 * line_draw)
    background = jnp.clip(0.3 * jax.random.normal(jax.random.fold_in(key, 2), shape, jnp.float32), -6.0, 6.0)
    return jnp.where(ridge, lines, background)


def draw_land_mask(key, part):
    return sea_grid(key)


def draw_fold_partner(key, part):
    return partner_grid(key)


def draw_east_faces(key, part):
    sea_mask = sea_grid(key).astype(jnp.float32)
    open_faces = sea_mask * jnp.roll(sea_mask, -1, axis=2)
    col_place = lax.broadcasted_iota(jnp.int32, (LEV, NLAT, NLON), 2) % CLON
    pinned = jnp.where((col_place == CLON - 3) | (col_place == CLON - 1), 1.0, 0.0).astype(jnp.float32)
    return face_numbers(key, 7003, open_faces, pinned)


def draw_north_faces(key, part):
    sea_mask = sea_grid(key).astype(jnp.float32)
    partner = partner_grid(key)
    top_wet = jnp.take(sea_mask[:, -1:, :], partner, axis=2)
    north_wet = jnp.concatenate([sea_mask[:, 1:, :], top_wet], axis=1)
    row_grid = lax.broadcasted_iota(jnp.int32, (LEV, NLAT, NLON), 1)
    row_place = row_grid % CLAT
    forward = jnp.where((row_place == CLAT - 3) | (row_place == CLAT - 1), 1.0, 0.0)
    pinned = jnp.where(row_grid == NLAT - 1, -1.0, forward).astype(jnp.float32)
    return face_numbers(key, 7005, sea_mask * north_wet, pinned)


def setup_inputs(seed: int = 0) -> dict:
    keys = jax.random.split(jax.random.key(seed), 7)
    return {
        "tracers": draw_tracers(jax.random.fold_in(keys[6], 71), 0),
        "east_faces": draw_east_faces(jax.random.fold_in(keys[6], 71), 0),
        "north_faces": draw_north_faces(jax.random.fold_in(keys[6], 71), 0),
        "land_mask": draw_land_mask(jax.random.fold_in(keys[6], 71), 0),
        "fold_partner": draw_fold_partner(jax.random.fold_in(keys[6], 71), 0),
        "vert_mix": jnp.clip(jnp.exp(jax.random.uniform(keys[5], (LEV - 1,), jnp.float32, math.log(0.05), math.log(0.3))), 0.05, 0.3),
    }


def quick_flux(c_minus, c_zero, c_plus, c_plus2, flow_number, spread_number):
    upwind = 0.75 * c_zero + 0.375 * c_plus - 0.125 * c_minus
    downwind = 0.75 * c_plus + 0.375 * c_zero - 0.125 * c_plus2
    return flow_number * jnp.where(flow_number > 0.0, upwind, downwind) - spread_number * (c_plus - c_zero)


def reference(tracers, east_faces, north_faces, land_mask, fold_partner, vert_mix):
    wet_cells = land_mask.astype(jnp.float32)
    vert_open = vert_mix[:, None, None] * wet_cells[:-1] * wet_cells[1:]
    east_all = jnp.concatenate([east_faces[..., -1:], east_faces], axis=3)
    south_zero = jnp.zeros_like(north_faces[:, :, :1, :])
    north_all = jnp.concatenate([south_zero, north_faces], axis=2)
    fields = tracers
    for turn_index in range(STEPS):
        fold_ghost = jnp.take(fields[:, :, NLAT - 2:, :][:, :, ::-1, :], fold_partner, axis=3)
        changes = []
        for level_index in range(LEV):
            layer = fields[:, level_index]
            lon_padded = jnp.concatenate([layer[..., -2:], layer, layer[..., :2]], axis=2)
            lat_padded = jnp.concatenate([jnp.zeros((2, 2, NLON), jnp.float32), layer, fold_ghost[:, level_index]], axis=1)
            flux_east = quick_flux(lon_padded[..., 0:NLON + 1], lon_padded[..., 1:NLON + 2], lon_padded[..., 2:NLON + 3], lon_padded[..., 3:NLON + 4], east_all[0, level_index], east_all[1, level_index])
            flux_north = quick_flux(lat_padded[:, 0:NLAT + 1], lat_padded[:, 1:NLAT + 2], lat_padded[:, 2:NLAT + 3], lat_padded[:, 3:NLAT + 4], north_all[0, level_index], north_all[1, level_index])
            changes.append((flux_east[..., :-1] - flux_east[..., 1:]) + (flux_north[:, :-1] - flux_north[:, 1:]))
        horizontal = jnp.stack(changes, axis=1)
        vertical = vert_open * (fields[:, 1:] - fields[:, :-1])
        zero_layer = jnp.zeros_like(fields[:, :1])
        change = horizontal + (jnp.concatenate([vertical, zero_layer], axis=1) - jnp.concatenate([zero_layer, vertical], axis=1))
        fields = fields + wet_cells * change
    potential = fields[0]
    salinity = fields[1]
    density = wet_cells * (0.8 * salinity - 0.2 * potential - 0.05 * potential * potential)
    return fields, density
```

```python
import jax
import jax.numpy as jnp
from jax import lax
from jax.experimental import pallas as pl
from jax.experimental.pallas import tpu as pltpu
from jax.sharding import PartitionSpec as P

F32 = jnp.float32
LANES = 128
SUB = 8
PAD = 8
TRACERS = 2
VMEM_BYTES = 48 * 1024 * 1024


def lane_ids():
    return lax.broadcasted_iota(jnp.int32, (SUB, LANES), 1)


def rolled(x, by):
    by = by % LANES
    return x if by == 0 else pltpu.roll(x, by, 1)


def face_terms(flow, spread):
    g = 0.125 * flow
    up = flow > 0.0
    g3 = 3.0 * g
    g6 = 6.0 * g
    return jnp.where(up, g6, g3) + spread, jnp.where(up, g3, g6) - spread, g, up


def tile_rows(index, offset=0):
    return pl.ds(pl.multiple_of(index * SUB, SUB) + offset, SUB)


def advance_tile(r, c, south, east, north, mask, mix, out, out_pad):
    levels = mask.shape[0]
    lane = lane_ids()
    first, last, last2 = lane > 0, lane < LANES - 1, lane < LANES - 2
    rows = tile_rows(r)
    wet = [mask[0, h, rows, :].astype(F32) for h in range(2)]
    below = [[None] * 2 for _ in range(TRACERS)]
    here = [[c[t, 0, h, tile_rows(r, PAD), :] for h in range(2)] for t in range(TRACERS)]
    for k in range(levels):
        if k + 1 < levels:
            wet_up = [mask[k + 1, h, rows, :].astype(F32) for h in range(2)]
            mixing = [mix[k] * wet[h] * wet_up[h] for h in range(2)]
            above = [[c[t, k + 1, h, tile_rows(r, PAD), :] for h in range(2)] for t in range(TRACERS)]
        east_terms = [face_terms(east[0, k, h, rows, :], east[1, k, h, rows, :]) for h in range(2)]
        north_terms = [face_terms(north[0, k, h, rows, :], north[1, k, h, rows, :]) for h in range(2)]
        for t in range(TRACERS):
            c0 = here[t][0], here[t][1]
            plus1 = [rolled(x, -1) for x in c0]
            plus2 = [rolled(x, -2) for x in c0]
            minus1 = [rolled(x, 1) for x in c0]
            p1 = jnp.where(last, plus1[0], plus1[1]), jnp.where(last, plus1[1], 0.0)
            p2 = jnp.where(last2, plus2[0], plus2[1]), jnp.where(last2, plus2[1], 0.0)
            m1 = jnp.where(first, minus1[0], 0.0), jnp.where(first, minus1[1], minus1[0])
            flux = []
            for h in range(2):
                a, b, g, up = east_terms[h]
                flux.append(a * c0[h] + b * p1[h] - g * jnp.where(up, m1[h], p2[h]))
            shifted = [rolled(x, 1) for x in flux]
            west = jnp.where(first, shifted[0], 0.0), jnp.where(first, shifted[1], shifted[0])
            for h in range(2):
                change = west[h] - flux[h]
                a, b, g, up = north_terms[h]
                further = jnp.where(
                    up,
                    c[t, k, h, tile_rows(r, PAD - 1), :],
                    c[t, k, h, tile_rows(r, PAD + 2), :],
                )
                face = a * c0[h] + b * c[t, k, h, tile_rows(r, PAD + 1), :] - g * further
                south[t, k, h, tile_rows(r, PAD), :] = face
                change = change + (south[t, k, h, tile_rows(r, PAD - 1), :] - face)
                if k + 1 < levels:
                    vertical = mixing[h] * (above[t][h] - c0[h])
                    change = change + vertical
                if k > 0:
                    change = change - below[t][h]
                if k + 1 < levels:
                    below[t][h] = vertical
                out[t, k, h, tile_rows(r, out_pad), :] = c0[h] + wet[h] * change
        if k + 1 < levels:
            wet = wet_up
            here = above


def slot_group(slot_lane, tl):
    return lax.shift_right_logical(slot_lane, 3) == tl


def packed_edges(get, levels):
    lane = lane_ids()
    west = jnp.zeros((SUB, LANES), F32)
    east = jnp.zeros((SUB, LANES), F32)
    for t in range(TRACERS):
        for k in range(levels):
            tl = t * levels + k
            inside = slot_group(lane, tl)
            west = jnp.where(inside, rolled(get(t, k, 0), 8 * tl), west)
            east = jnp.where(inside, rolled(get(t, k, 1), 8 * tl + 2), east)
    return west, east


def parity(axis):
    return lax.rem(lax.axis_index(axis), 2) == 0


def start_kernel(tracers, east, north, c, side_a, side_b, rows_a, rows_b, east_last, north_top, sems):
    levels, tall = tracers.shape[1], tracers.shape[2]
    tiles = tall // SUB
    cuts = [0, 40, 80, 120, tall]
    copies = []
    for i, (lo, hi) in enumerate(zip(cuts[:-1], cuts[1:])):
        group = []
        for h in range(2):
            group.append(
                pltpu.make_async_copy(
                    tracers.at[:, :, lo:hi, h * LANES : (h + 1) * LANES],
                    c.at[:, :, h, PAD + lo : PAD + hi, :],
                    sems.at[3 * i + h],
                )
            )
        group.append(
            pltpu.make_async_copy(
                east.at[:, :, lo:hi, LANES:], east_last.at[:, :, lo:hi, :], sems.at[3 * i + 2]
            )
        )
        copies.append(group)
    top_copy = pltpu.make_async_copy(north.at[:, :, tall - SUB :, :], north_top, sems.at[12])
    for group in copies:
        for one in group:
            one.start()
    top_copy.start()
    for t in range(TRACERS):
        for k in range(levels):
            for h in range(2):
                c[t, k, h, 0:PAD, :] = jnp.zeros((PAD, LANES), F32)
                c[t, k, h, PAD + tall :, :] = jnp.zeros((PAD, LANES), F32)
    lane = lane_ids()
    even_lon = parity("lon")

    def pack(r, carry):
        rows = tile_rows(r)
        faces = []
        for k in range(levels):
            flow = rolled(east_last[0, k, rows, :], 1)
            spread = rolled(east_last[1, k, rows, :], 2)
            faces.append(jnp.where(lane == 0, flow, spread))

        def get(t, k, h):
            x = c[t, k, h, tile_rows(r, PAD), :]
            return jnp.where(lane >= LANES - 2, x, faces[k]) if h == 1 else x

        west, east_side = packed_edges(get, levels)
        side_a[rows, :] = jnp.where(even_lon, east_side, west)
        side_b[rows, :] = jnp.where(even_lon, west, east_side)
        return carry

    for i, (lo, hi) in enumerate(zip(cuts[:-1], cuts[1:])):
        for one in copies[i]:
            one.wait()
        lax.fori_loop(lo // SUB, hi // SUB, pack, 0)
    top_copy.wait()
    send_rows(c, rows_a, rows_b, levels, tall)
    for comp in range(2):
        for k in range(levels):
            one_row = north_top[comp, k, SUB - 1 : SUB, :]
            at = 2 * TRACERS * levels + comp * levels + k
            rows_a[at : at + 1, :] = one_row
            rows_b[at : at + 1, :] = one_row


def send_rows(c, rows_a, rows_b, levels, tall):
    even_lat = parity("lat")
    for depth in range(2):
        top, bottom = PAD + tall - 1 - depth, PAD + depth
        at_a = jnp.where(even_lat, top, bottom)
        at_b = jnp.where(even_lat, bottom, top)
        for t in range(TRACERS):
            for k in range(levels):
                tl = (depth * TRACERS + t) * levels + k
                for h in range(2):
                    cols = slice(h * LANES, (h + 1) * LANES)
                    rows_a[tl : tl + 1, cols] = c[t, k, h, pl.ds(at_a, 1), :]
                    rows_b[tl : tl + 1, cols] = c[t, k, h, pl.ds(at_b, 1), :]


def inner_kernel(c, east, north, mask, mix, out, packed, own, row_own, east_in, north_in, mask_in, south, sems):
    levels, tall = mask.shape[0], mask.shape[1]
    cuts = [0, 24, 64, 104, tall]
    copies = []
    for i, (lo, hi) in enumerate(zip(cuts[:-1], cuts[1:])):
        group = []
        for h in range(2):
            cols = slice(h * LANES, (h + 1) * LANES)
            for j, (src, dst) in enumerate(((east, east_in), (north, north_in))):
                group.append(
                    pltpu.make_async_copy(
                        src.at[:, :, lo:hi, cols], dst.at[:, :, h, lo:hi, :], sems.at[6 * i + 3 * h + j]
                    )
                )
            group.append(
                pltpu.make_async_copy(
                    mask.at[:, lo:hi, cols], mask_in.at[:, h, lo:hi, :], sems.at[6 * i + 3 * h + 2]
                )
            )
        copies.append(group)
    for group in copies:
        for one in group:
            one.start()
    for t in range(TRACERS):
        for k in range(levels):
            for h in range(2):
                south[t, k, h, 0:PAD, :] = jnp.zeros((PAD, LANES), F32)
                out[t, k, h, 0:PAD, :] = jnp.zeros((PAD, LANES), F32)
                out[t, k, h, PAD + tall :, :] = jnp.zeros((PAD, LANES), F32)
    lane = lane_ids()

    def body(r, carry):
        rows = tile_rows(r)
        advance_tile(r, c, south, east_in, north_in, mask_in, mix, out, PAD)
        west, last = packed_edges(lambda t, k, h: out[t, k, h, tile_rows(r, PAD), :], levels)
        packed[0, rows, :] = west
        packed[1, rows, :] = last
        kept = jnp.zeros((SUB, LANES), F32)
        for k in range(levels):
            wet0 = mask_in[k, 0, rows, :].astype(F32)
            wet1 = mask_in[k, 1, rows, :].astype(F32)
            flow1 = east_in[0, k, 1, rows, :]
            one = jnp.where(lane == 0, east_in[0, k, 0, rows, :], rolled(wet0, 1))
            one = jnp.where(lane >= 3, rolled(flow1, 5), one)
            one = jnp.where(lane >= 5, rolled(east_in[1, k, 1, rows, :], 6), one)
            one = jnp.where(lane >= 6, rolled(wet1, 8), one)
            for t in range(TRACERS):
                tl = t * levels + k
                kept = jnp.where(slot_group(lane, tl), rolled(one, 8 * tl), kept)
        own[rows, :] = kept
        return carry

    for i, (lo, hi) in enumerate(zip(cuts[:-1], cuts[1:])):
        for one in copies[i]:
            one.wait()
        lax.fori_loop(lo // SUB, hi // SUB, body, 0)
    for k in range(levels):
        for h in range(2):
            cols = slice(h * LANES, (h + 1) * LANES)
            kept_rows = (
                north_in[0, k, h, 0:1, :],
                north_in[0, k, h, tall - 2 : tall - 1, :],
                north_in[0, k, h, tall - 1 : tall, :],
                north_in[1, k, h, tall - 1 : tall, :],
                mask_in[k, h, 0:1, :].astype(F32),
                mask_in[k, h, 1:2, :].astype(F32),
                mask_in[k, h, tall - 2 : tall - 1, :].astype(F32),
                mask_in[k, h, tall - 1 : tall, :].astype(F32),
            )
            for j, one in enumerate(kept_rows):
                row_own[j * levels + k : j * levels + k + 1, cols] = one


def side_correction(west, east, mine, own):
    lane = lax.bitwise_and(lane_ids(), 7)
    a, b, g, up = face_terms(rolled(west, -2), rolled(west, -3))
    near = rolled(west, -1)
    flux = a * near + b * mine - g * jnp.where(up, west, rolled(mine, -1))
    first = jnp.maximum(0.125 * own, 0.0) * near
    col0 = rolled(own, -1) * (flux + first)
    col1 = -(rolled(own, -2) * first)
    a, b, g, up = face_terms(rolled(own, -4), rolled(own, -5))
    last = b * east - jnp.minimum(g, 0.0) * rolled(east, -1)
    before = -(jnp.minimum(0.125 * rolled(own, -3), 0.0) * east)
    col2 = -(rolled(own, -6) * before)
    col3 = rolled(own, -7) * (before - last)
    found = jnp.where(lane == 0, col0, rolled(col1, 1))
    found = jnp.where(lane >= 2, rolled(col2, 2), found)
    found = jnp.where(lane >= 3, rolled(col3, 3), found)
    return jnp.where(lane < 4, found, 0.0)


def unpacked(correction, tl, h):
    lane = lane_ids()
    if h == 0:
        return jnp.where(lane < 2, rolled(correction, -8 * tl), 0.0)
    return jnp.where(lane >= LANES - 2, rolled(correction, LANES - 4 - 8 * tl), 0.0)


def across_fold(x, index):
    picked = []
    for h in range(2):
        at = jnp.broadcast_to(index[:, h * LANES : (h + 1) * LANES], (SUB, LANES))
        low = lax.bitwise_and(at, LANES - 1)
        parts = [jnp.take_along_axis(x[j], low, axis=1) for j in range(2)]
        picked.append(jnp.where(at < LANES, parts[0], parts[1]))
    return picked


def row_corrections(state, offset, rows_a, rows_b, faces_a, faces_b, row_own, index, tall, levels, apply):
    even_lat = parity("lat")
    lat = lax.axis_index("lat")
    at_top = lat == lax.axis_size("lat") - 1
    at_bottom = lat == 0
    for t in range(TRACERS):
        part = [slice((depth * TRACERS + t) * levels, (depth * TRACERS + t + 1) * levels) for depth in range(2)]
        north, south = [], []
        for depth in range(2):
            one, other = rows_a[part[depth], :], rows_b[part[depth], :]
            upper = jnp.where(even_lat, one, other)
            lower = jnp.where(even_lat, other, one)
            lower = jnp.where(at_bottom, 0.0, lower)
            upper = [upper[:, h * LANES : (h + 1) * LANES] for h in range(2)]
            folded = across_fold(upper, index)
            north.append([jnp.where(at_top, folded[h], upper[h]) for h in range(2)])
            south.append([lower[:, h * LANES : (h + 1) * LANES] for h in range(2)])
        for h in range(2):
            cols = slice(h * LANES, (h + 1) * LANES)
            base = 2 * TRACERS * levels
            faces = []
            for comp in range(2):
                span = slice(base + comp * levels, base + (comp + 1) * levels)
                one = jnp.where(even_lat, faces_b[span, cols], faces_a[span, cols])
                faces.append(jnp.where(at_bottom, 0.0, one))
            kept = [row_own[j * levels : (j + 1) * levels, cols] for j in range(8)]
            bottom = [
                jnp.concatenate([state[t, k, h, offset + j : offset + j + 1, :] for k in range(levels)], axis=0)
                for j in range(2)
            ]
            a, b, g, up = face_terms(faces[0], faces[1])
            flux = a * south[0][h] + b * bottom[0] - g * jnp.where(up, south[1][h], bottom[1])
            first = jnp.maximum(0.125 * kept[0], 0.0) * south[0][h]
            row0 = kept[4] * (flux + first)
            row1 = -(kept[5] * first)
            a, b, g, up = face_terms(kept[2], kept[3])
            last = b * north[0][h] - jnp.minimum(g, 0.0) * north[1][h]
            before = -(jnp.minimum(0.125 * kept[1], 0.0) * north[0][h])
            row2 = -(kept[6] * before)
            row3 = kept[7] * (before - last)
            for k in range(levels):
                for at, add in ((0, row0), (1, row1), (tall - 2, row2), (tall - 1, row3)):
                    apply(t, k, h, at, add[k : k + 1, :])


def received(side_a, side_b, rows, even_lon):
    one, other = side_a[rows, :], side_b[rows, :]
    return jnp.where(even_lon, other, one), jnp.where(even_lon, one, other)


def add_rows(state, offset):
    def apply(t, k, h, at, add):
        spot = (t, k, h, slice(offset + at, offset + at + 1), slice(None))
        state[spot] = state[spot] + add

    return apply


def edge_kernel(
    got_a, got_b, sent_a, sent_b, rows_a, rows_b, own, row_own, packed, index, before, c_in,
    c, next_a, next_b, next_rows_a, next_rows_b, correction,
):
    levels, tall = before.shape[1], own.shape[0]
    tiles = tall // SUB
    even_lon = parity("lon")

    def one_tile(r):
        rows = tile_rows(r)
        west, east = received(got_a, got_b, rows, even_lon)
        _, mine = received(sent_a, sent_b, rows, jnp.logical_not(even_lon))
        return side_correction(west, east, mine, own[rows, :])

    def middle(r, carry):
        rows = tile_rows(r)
        found = one_tile(r)
        correction[rows, :] = found
        west = packed[0, rows, :] + found
        east = packed[1, rows, :] + rolled(found, -2)
        next_a[rows, :] = jnp.where(even_lon, east, west)
        next_b[rows, :] = jnp.where(even_lon, west, east)
        return carry

    lax.fori_loop(1, tiles - 1, middle, 0)
    row_corrections(before, PAD, rows_a, rows_b, rows_a, rows_b, row_own, index, tall, levels, add_rows(c, PAD))
    for r in (0, tiles - 1):
        rows = tile_rows(r)
        found = one_tile(r)
        correction[rows, :] = jnp.zeros((SUB, LANES), F32)
        for t in range(TRACERS):
            for k in range(levels):
                for h in range(2):
                    spot = (t, k, h, tile_rows(r, PAD), slice(None))
                    c[spot] = c[spot] + unpacked(found, t * levels + k, h)
        west, east = packed_edges(lambda t, k, h: c[t, k, h, tile_rows(r, PAD), :], levels)
        next_a[rows, :] = jnp.where(even_lon, east, west)
        next_b[rows, :] = jnp.where(even_lon, west, east)
    send_rows(c, next_rows_a, next_rows_b, levels, tall)


def second_kernel(c_in, correction, east_in, north_in, mask_in, mix, c, out, south):
    levels, tall = mask_in.shape[0], mask_in.shape[2]
    tiles = tall // SUB
    for t in range(TRACERS):
        for k in range(levels):
            for h in range(2):
                south[t, k, h, 0:PAD, :] = jnp.zeros((PAD, LANES), F32)

    def fix(r):
        found = correction[tile_rows(r), :]
        for t in range(TRACERS):
            for k in range(levels):
                for h in range(2):
                    spot = (t, k, h, tile_rows(r, PAD), slice(None))
                    c[spot] = c[spot] + unpacked(found, t * levels + k, h)

    def body(r, carry):
        fix(r + 1)
        advance_tile(r, c, south, east_in, north_in, mask_in, mix, out, 0)
        return carry

    lax.fori_loop(0, tiles - 1, body, 0)
    advance_tile(tiles - 1, c, south, east_in, north_in, mask_in, mix, out, 0)


def last_kernel(
    got_a, got_b, sent_a, sent_b, first_a, first_b, rows_a, rows_b, faces_a, faces_b,
    own, row_own, index, before, mask_in, c_in,
    fields, density, c, fields_out, density_out, sems,
):
    levels, tall = before.shape[1], own.shape[0]
    even_lon = parity("lon")
    slot = lax.bitwise_and(lane_ids(), 7)
    row_corrections(before, PAD, rows_a, rows_b, faces_a, faces_b, row_own, index, tall, levels, add_rows(c, 0))

    def body(r, carry):
        rows = tile_rows(r)
        west, east = received(got_a, got_b, rows, even_lon)
        earlier, _ = received(first_a, first_b, rows, even_lon)
        west = jnp.where(slot < 2, west, earlier)
        _, mine = received(sent_a, sent_b, rows, jnp.logical_not(even_lon))
        found = side_correction(west, east, mine, own[rows, :])
        for k in range(levels):
            for h in range(2):
                both = []
                for t in range(TRACERS):
                    x = c[t, k, h, rows, :] + unpacked(found, t * levels + k, h)
                    fields_out[t, k, h, rows, :] = x
                    both.append(x)
                heat, salt = both
                wet = mask_in[k, h, rows, :].astype(F32)
                density_out[k, h, rows, :] = wet * (0.8 * salt - 0.2 * heat - 0.05 * heat * heat)
        return carry

    cuts = [0, 40, 80, 120, tall]
    copies = []
    for i, (lo, hi) in enumerate(zip(cuts[:-1], cuts[1:])):
        lax.fori_loop(lo // SUB, hi // SUB, body, 0)
        for h in range(2):
            cols = slice(h * LANES, (h + 1) * LANES)
            copies.append(
                pltpu.make_async_copy(
                    fields_out.at[:, :, h, lo:hi, :], fields.at[:, :, lo:hi, cols], sems.at[4 * i + h]
                )
            )
            copies.append(
                pltpu.make_async_copy(
                    density_out.at[:, h, lo:hi, :], density.at[:, lo:hi, cols], sems.at[4 * i + 2 + h]
                )
            )
        for one in copies[-4:]:
            one.start()
    for one in copies:
        one.wait()


def vmem(*shape, dtype=F32):
    return pltpu.VMEM(shape, dtype)


ON_CHIP = pl.BlockSpec(memory_space=pltpu.VMEM)
ANYWHERE = pl.BlockSpec(memory_space=pl.ANY)
SCALARS = pl.BlockSpec(memory_space=pltpu.SMEM)


def call(kernel, ins, out_shape, out_specs, scratch, cost, aliases=None):
    return pl.pallas_call(
        kernel,
        out_shape=out_shape,
        in_specs=ins,
        out_specs=out_specs,
        scratch_shapes=scratch,
        input_output_aliases=aliases or {},
        cost_estimate=pl.CostEstimate(flops=cost[0], bytes_accessed=cost[1], transcendentals=0),
        compiler_params=pltpu.CompilerParams(vmem_limit_bytes=VMEM_BYTES),
    )


def pairings(lats, lons):
    place = lambda a, o: (a % lats) * lons + o % lons
    by = {"lon_a": [], "lon_b": [], "lat_a": [], "lat_b": []}
    for a in range(lats):
        for o in range(lons):
            me = place(a, o)
            by["lon_a"].append((me, place(a, o ^ 1)))
            by["lon_b"].append((me, place(a, o + 1 if o % 2 else o - 1)))
            by["lat_a"].append((me, place(a ^ 1, o)))
            if a == lats - 1:
                other = place(a, lons - 1 - o)
            elif a == 0:
                other = place(a, o ^ 1)
            else:
                other = place(a + 1 if a % 2 else a - 1, o)
            by["lat_b"].append((me, other))
    return by


def on_device(pairs, tracers, east_faces, north_faces, land_mask, fold_partner, vert_mix):
    _, levels, tall, wide = tracers.shape
    assert wide == 2 * LANES and TRACERS * levels * 8 == LANES and tall % SUB == 0
    index = (fold_partner & (wide - 1)).reshape(1, wide)
    both = ("lat", "lon")
    swap = lambda x, name: lax.ppermute(x, both, pairs[name])
    state = vmem(TRACERS, levels, 2, tall + 2 * PAD, LANES)
    side, rows3, rows2 = vmem(tall, LANES), vmem(6 * levels, wide), vmem(4 * levels, wide)
    faces = vmem(2, levels, 2, tall, LANES)
    mask_shape = vmem(levels, 2, tall, LANES, dtype=jnp.int32)
    grid_bytes = tracers.size * 4

    c0, side_a, side_b, rows_a, rows_b = call(
        start_kernel,
        [ANYWHERE] * 3,
        [state, side, side, rows3, rows3],
        [ON_CHIP] * 5,
        [vmem(2, levels, tall, LANES), vmem(2, levels, SUB, wide), pltpu.SemaphoreType.DMA((13,))],
        (1000000, 2 * grid_bytes),
    )(tracers, east_faces, north_faces)
    got_a, got_b = swap(side_a, "lon_a"), swap(side_b, "lon_b")
    got_rows_a, got_rows_b = swap(rows_a, "lat_a"), swap(rows_b, "lat_b")
    c1, packed, own, row_own, east_in, north_in, mask_in = call(
        inner_kernel,
        [ON_CHIP, ANYWHERE, ANYWHERE, ANYWHERE, SCALARS],
        [state, vmem(2, tall, LANES), side, vmem(8 * levels, wide), faces, faces, mask_shape],
        [ON_CHIP] * 7,
        [vmem(TRACERS, levels, 2, tall + PAD, LANES), pltpu.SemaphoreType.DMA((24,))],
        (40000000, 4 * grid_bytes),
    )(c0, east_faces, north_faces, land_mask, vert_mix)
    c1, next_a, next_b, next_rows_a, next_rows_b, correction = call(
        edge_kernel,
        [ON_CHIP] * 12,
        [state, side, side, rows2, rows2, side],
        [ON_CHIP] * 6,
        [],
        (1000000, 1000000),
        {11: 0},
    )(got_a, got_b, side_a, side_b, got_rows_a, got_rows_b, own, row_own, packed, index, c0, c1)
    new_a, new_b = swap(next_a, "lon_a"), swap(next_b, "lon_b")
    new_rows_a, new_rows_b = swap(next_rows_a, "lat_a"), swap(next_rows_b, "lat_b")
    c1, c2 = call(
        second_kernel,
        [ON_CHIP] * 5 + [SCALARS],
        [state, vmem(TRACERS, levels, 2, tall, LANES)],
        [ON_CHIP] * 2,
        [vmem(TRACERS, levels, 2, tall + PAD, LANES)],
        (40000000, 4 * grid_bytes),
        {0: 0},
    )(c1, correction, east_in, north_in, mask_in, vert_mix)
    fields, density, _ = call(
        last_kernel,
        [ON_CHIP] * 16,
        [
            jax.ShapeDtypeStruct(tracers.shape, F32),
            jax.ShapeDtypeStruct(land_mask.shape, F32),
            vmem(TRACERS, levels, 2, tall, LANES),
        ],
        [ANYWHERE, ANYWHERE, ON_CHIP],
        [
            vmem(TRACERS, levels, 2, tall, LANES),
            vmem(levels, 2, tall, LANES),
            pltpu.SemaphoreType.DMA((16,)),
        ],
        (4000000, 2 * grid_bytes),
        {15: 2},
    )(
        new_a, new_b, next_a, next_b, got_a, got_b, new_rows_a, new_rows_b, got_rows_a, got_rows_b,
        own, row_own, index, c1, mask_in, c2,
    )
    return fields, density


def solution(mesh):
    in_specs = (
        P(None, None, "lat", "lon"),
        P(None, None, "lat", "lon"),
        P(None, None, "lat", "lon"),
        P(None, "lat", "lon"),
        P("lon"),
        P(),
    )
    out_specs = (P(None, None, "lat", "lon"), P(None, "lat", "lon"))
    pairs = pairings(mesh.shape["lat"], mesh.shape["lon"])

    def body(*args):
        return on_device(pairs, *args)

    return jax.shard_map(body, mesh=mesh, in_specs=in_specs, out_specs=out_specs, check_vma=False)
```

```python
import jax
import jax.numpy as jnp
from jax import lax
from jax.experimental import pallas as pl
from jax.experimental.pallas import tpu as pltpu
from jax.sharding import PartitionSpec as P

F32 = jnp.float32
LANES = 128
SUB = 8
PAD = 8
TRACERS = 2
VMEM_BYTES = 12 * 1024 * 1024


def lane_ids():
    return lax.broadcasted_iota(jnp.int32, (SUB, LANES), 1)


def rolled(x, by):
    by = by % LANES
    return x if by == 0 else pltpu.roll(x, by, 1)


def face_terms(flow, spread):
    g = 0.125 * flow
    up = flow > 0.0
    g3 = 3.0 * g
    g6 = 6.0 * g
    return jnp.where(up, g6, g3) + spread, jnp.where(up, g3, g6) - spread, g, up


def tile_rows(index, offset=0):
    return pl.ds(pl.multiple_of(index * SUB, SUB) + offset, SUB)


def set_terms(r, east, north, mask, mix, terms, wet, mixing):
    levels = wet.shape[0]
    rows = tile_rows(r)
    for h in range(2):
        cells = [mask[k, h, rows, :].astype(F32) for k in range(levels)]
        for k in range(levels):
            wet[k, h, rows, :] = cells[k]
            if k + 1 < levels:
                mixing[k, h, rows, :] = mix[k] * cells[k] * cells[k + 1]
            for way, faces in enumerate((east, north)):
                a, b, g, _ = face_terms(faces[0, k, h, rows, :], faces[1, k, h, rows, :])
                for j, one in enumerate((a, b, g)):
                    terms[way, j, k, h, rows, :] = one


def advance_tile(r, c, south, terms, wet, mixing, out, out_pad):
    levels = wet.shape[0]
    lane = lane_ids()
    first, last, last2 = lane > 0, lane < LANES - 1, lane < LANES - 2
    rows = tile_rows(r)

    def cells(t, k, h, by=0):
        return c[t, k, h, tile_rows(r, PAD + by), :]

    for k in range(levels):
        for h in range(2):
            a, b, g = (terms[1, j, k, h, rows, :] for j in range(3))
            up = g > 0.0
            for t in range(TRACERS):
                further = jnp.where(up, cells(t, k, h, -1), cells(t, k, h, 2))
                face = a * cells(t, k, h) + b * cells(t, k, h, 1) - g * further
                south[t, k, h, tile_rows(r, PAD), :] = face
    below = [[None] * 2 for _ in range(TRACERS)]
    for k in range(levels):
        for t in range(TRACERS):
            c0 = [cells(t, k, h) for h in range(2)]
            plus1 = [rolled(x, -1) for x in c0]
            plus2 = [rolled(x, -2) for x in c0]
            minus1 = [rolled(x, 1) for x in c0]
            p1 = jnp.where(last, plus1[0], plus1[1]), jnp.where(last, plus1[1], 0.0)
            p2 = jnp.where(last2, plus2[0], plus2[1]), jnp.where(last2, plus2[1], 0.0)
            m1 = jnp.where(first, minus1[0], 0.0), jnp.where(first, minus1[1], minus1[0])
            flux = []
            for h in range(2):
                a, b, g = (terms[0, j, k, h, rows, :] for j in range(3))
                flux.append(a * c0[h] + b * p1[h] - g * jnp.where(g > 0.0, m1[h], p2[h]))
            shifted = [rolled(x, 1) for x in flux]
            west = jnp.where(first, shifted[0], 0.0), jnp.where(first, shifted[1], shifted[0])
            for h in range(2):
                change = west[h] - flux[h]
                change = change + (south[t, k, h, tile_rows(r, PAD - 1), :] - south[t, k, h, tile_rows(r, PAD), :])
                if k + 1 < levels:
                    vertical = mixing[k, h, rows, :] * (cells(t, k + 1, h) - c0[h])
                    change = change + vertical
                if k > 0:
                    change = change - below[t][h]
                if k + 1 < levels:
                    below[t][h] = vertical
                out[t, k, h, tile_rows(r, out_pad), :] = c0[h] + wet[k, h, rows, :] * change


def group(tl):
    lane = lane_ids()
    return lax.bitwise_and(lax.shift_right_logical(lane + 2, 3), LANES // SUB - 1) == tl


def slots():
    return lax.bitwise_and(lane_ids() + 2, 7) - 2


def packed_edges(get, levels, extra=None):
    lane = lane_ids()
    packed = jnp.zeros((SUB, LANES), F32)
    for t in range(TRACERS):
        for k in range(levels):
            tl = t * levels + k
            one = jnp.where(lane >= LANES - 2, get(t, k, 1), get(t, k, 0))
            if extra is not None:
                one = jnp.where(jnp.logical_and(lane >= 2, lane < 4), extra[k], one)
            packed = jnp.where(group(tl), rolled(one, 8 * tl), packed)
    return packed


def parity(axis):
    return lax.rem(lax.axis_index(axis), 2) == 0


def start_kernel(tracers, east, north, c, side, rows_a, rows_b, east_last, north_top, sems):
    levels, tall = tracers.shape[1], tracers.shape[2]
    cuts = [0, 40, 80, 120, tall]
    copies = []
    for i, (lo, hi) in enumerate(zip(cuts[:-1], cuts[1:])):
        group_of = []
        for h in range(2):
            group_of.append(
                pltpu.make_async_copy(
                    tracers.at[:, :, lo:hi, h * LANES : (h + 1) * LANES],
                    c.at[:, :, h, PAD + lo : PAD + hi, :],
                    sems.at[3 * i + h],
                )
            )
        group_of.append(
            pltpu.make_async_copy(
                east.at[:, :, lo:hi, LANES:], east_last.at[:, :, lo:hi, :], sems.at[3 * i + 2]
            )
        )
        copies.append(group_of)
    top_copy = pltpu.make_async_copy(north.at[:, :, tall - SUB :, :], north_top, sems.at[12])
    for group_of in copies:
        for one in group_of:
            one.start()
    top_copy.start()
    for t in range(TRACERS):
        for k in range(levels):
            for h in range(2):
                c[t, k, h, 0:PAD, :] = jnp.zeros((PAD, LANES), F32)
                c[t, k, h, PAD + tall :, :] = jnp.zeros((PAD, LANES), F32)
    lane = lane_ids()

    def pack(r, carry):
        rows = tile_rows(r)
        faces = []
        for k in range(levels):
            faces.append(
                jnp.where(lane == 2, rolled(east_last[0, k, rows, :], 3), rolled(east_last[1, k, rows, :], 4))
            )
        side[rows, :] = packed_edges(lambda t, k, h: c[t, k, h, tile_rows(r, PAD), :], levels, faces)
        return carry

    for i, (lo, hi) in enumerate(zip(cuts[:-1], cuts[1:])):
        for one in copies[i]:
            one.wait()
        lax.fori_loop(lo // SUB, hi // SUB, pack, 0)
    top_copy.wait()
    send_rows(c, rows_a, rows_b, levels, tall)
    for comp in range(2):
        for k in range(levels):
            one_row = north_top[comp, k, SUB - 1 : SUB, :]
            at = 2 * TRACERS * levels + comp * levels + k
            rows_a[at : at + 1, :] = one_row
            rows_b[at : at + 1, :] = one_row


def send_rows(c, rows_a, rows_b, levels, tall):
    even_lat = parity("lat")
    for depth in range(2):
        top, bottom = PAD + tall - 1 - depth, PAD + depth
        at_a = jnp.where(even_lat, top, bottom)
        at_b = jnp.where(even_lat, bottom, top)
        for t in range(TRACERS):
            for k in range(levels):
                tl = (depth * TRACERS + t) * levels + k
                for h in range(2):
                    cols = slice(h * LANES, (h + 1) * LANES)
                    rows_a[tl : tl + 1, cols] = c[t, k, h, pl.ds(at_a, 1), :]
                    rows_b[tl : tl + 1, cols] = c[t, k, h, pl.ds(at_b, 1), :]


def inner_kernel(c, east, north, mask, mix, out, packed, own, row_own, terms, wet, mixing, east_in, north_in, mask_in, south, sems):
    levels, tall = mask.shape[0], mask.shape[1]
    cuts = [0, 24, 64, 104, tall]
    copies = []
    for i, (lo, hi) in enumerate(zip(cuts[:-1], cuts[1:])):
        group_of = []
        for h in range(2):
            cols = slice(h * LANES, (h + 1) * LANES)
            for j, (src, dst) in enumerate(((east, east_in), (north, north_in))):
                group_of.append(
                    pltpu.make_async_copy(
                        src.at[:, :, lo:hi, cols], dst.at[:, :, h, lo:hi, :], sems.at[6 * i + 3 * h + j]
                    )
                )
            group_of.append(
                pltpu.make_async_copy(
                    mask.at[:, lo:hi, cols], mask_in.at[:, h, lo:hi, :], sems.at[6 * i + 3 * h + 2]
                )
            )
        copies.append(group_of)
    for group_of in copies:
        for one in group_of:
            one.start()
    for t in range(TRACERS):
        for k in range(levels):
            for h in range(2):
                south[t, k, h, 0:PAD, :] = jnp.zeros((PAD, LANES), F32)
                out[t, k, h, 0:PAD, :] = jnp.zeros((PAD, LANES), F32)
                out[t, k, h, PAD + tall :, :] = jnp.zeros((PAD, LANES), F32)
    lane = lane_ids()

    def body(r, carry):
        rows = tile_rows(r)
        set_terms(r, east_in, north_in, mask_in, mix, terms, wet, mixing)
        advance_tile(r, c, south, terms, wet, mixing, out, PAD)
        packed[rows, :] = packed_edges(lambda t, k, h: out[t, k, h, tile_rows(r, PAD), :], levels)
        kept = jnp.zeros((SUB, LANES), F32)
        edge = lane >= LANES - 2
        for k in range(levels):
            one = jnp.where(edge, wet[k, 1, rows, :], wet[k, 0, rows, :])
            flow = jnp.where(edge, east_in[0, k, 1, rows, :], east_in[0, k, 0, rows, :])
            some = jnp.where(lane == 5, rolled(east_in[1, k, 1, rows, :], 6), rolled(flow, 4))
            one = jnp.where(jnp.logical_and(lane >= 2, lane < 6), some, one)
            kept = jnp.where(group(k), rolled(one, 8 * k), kept)
        own[rows, :] = jnp.where(
            jnp.logical_or(lane < LANES // 2 - 2, edge), kept, rolled(kept, LANES // 2)
        )
        return carry

    for i, (lo, hi) in enumerate(zip(cuts[:-1], cuts[1:])):
        for one in copies[i]:
            one.wait()
        lax.fori_loop(lo // SUB, hi // SUB, body, 0)
    for k in range(levels):
        for h in range(2):
            cols = slice(h * LANES, (h + 1) * LANES)
            kept_rows = (
                north_in[0, k, h, 0:1, :],
                north_in[0, k, h, tall - 2 : tall - 1, :],
                north_in[0, k, h, tall - 1 : tall, :],
                north_in[1, k, h, tall - 1 : tall, :],
                wet[k, h, 0:1, :],
                wet[k, h, 1:2, :],
                wet[k, h, tall - 2 : tall - 1, :],
                wet[k, h, tall - 1 : tall, :],
            )
            for j, one in enumerate(kept_rows):
                row_own[j * levels + k : j * levels + k + 1, cols] = one


def side_correction(west, east, faces, mine, own):
    slot = slots()
    a, b, g, up = face_terms(rolled(faces, -2), rolled(faces, -3))
    near = rolled(west, 1)
    flux = a * near + b * mine - g * jnp.where(up, rolled(west, 2), rolled(mine, -1))
    flow = 0.125 * rolled(own, -4)
    first = jnp.maximum(flow, 0.0) * near
    _, b, _, _ = face_terms(rolled(own, -4), rolled(own, -6))
    beyond = jnp.minimum(flow, 0.0) * rolled(east, -2)
    last = rolled(beyond, 1) + b * rolled(east, -1)
    found = jnp.where(slot == 0, flux + first, -rolled(first, 1))
    found = jnp.where(slot < 0, beyond - jnp.where(slot == -1, last, 0.0), found)
    return jnp.where(slot < 2, own * found, 0.0)


def add_sides(get, correction, tl):
    lane = lane_ids()
    here = rolled(correction, -8 * tl)
    return get(0) + jnp.where(lane < 2, here, 0.0), get(1) + jnp.where(lane >= LANES - 2, here, 0.0)


def across_fold(x, index):
    picked = []
    for h in range(2):
        at = jnp.broadcast_to(index[:, h * LANES : (h + 1) * LANES], (SUB, LANES))
        low = lax.bitwise_and(at, LANES - 1)
        parts = [jnp.take_along_axis(x[j], low, axis=1) for j in range(2)]
        picked.append(jnp.where(at < LANES, parts[0], parts[1]))
    return picked


def row_corrections(state, offset, rows_a, rows_b, faces_a, faces_b, row_own, index, tall, levels, apply):
    even_lat = parity("lat")
    lat = lax.axis_index("lat")
    at_top = lat == lax.axis_size("lat") - 1
    at_bottom = lat == 0
    for t in range(TRACERS):
        part = [slice((depth * TRACERS + t) * levels, (depth * TRACERS + t + 1) * levels) for depth in range(2)]
        north, south = [], []
        for depth in range(2):
            one, other = rows_a[part[depth], :], rows_b[part[depth], :]
            upper = jnp.where(even_lat, one, other)
            lower = jnp.where(even_lat, other, one)
            lower = jnp.where(at_bottom, 0.0, lower)
            upper = [upper[:, h * LANES : (h + 1) * LANES] for h in range(2)]
            folded = across_fold(upper, index)
            north.append([jnp.where(at_top, folded[h], upper[h]) for h in range(2)])
            south.append([lower[:, h * LANES : (h + 1) * LANES] for h in range(2)])
        for h in range(2):
            cols = slice(h * LANES, (h + 1) * LANES)
            base = 2 * TRACERS * levels
            faces = []
            for comp in range(2):
                span = slice(base + comp * levels, base + (comp + 1) * levels)
                one = jnp.where(even_lat, faces_b[span, cols], faces_a[span, cols])
                faces.append(jnp.where(at_bottom, 0.0, one))
            kept = [row_own[j * levels : (j + 1) * levels, cols] for j in range(8)]
            bottom = [
                jnp.concatenate([state[t, k, h, offset + j : offset + j + 1, :] for k in range(levels)], axis=0)
                for j in range(2)
            ]
            a, b, g, up = face_terms(faces[0], faces[1])
            flux = a * south[0][h] + b * bottom[0] - g * jnp.where(up, south[1][h], bottom[1])
            first = jnp.maximum(0.125 * kept[0], 0.0) * south[0][h]
            row0 = kept[4] * (flux + first)
            row1 = -(kept[5] * first)
            a, b, g, up = face_terms(kept[2], kept[3])
            last = b * north[0][h] - jnp.minimum(g, 0.0) * north[1][h]
            before = -(jnp.minimum(0.125 * kept[1], 0.0) * north[0][h])
            row2 = -(kept[6] * before)
            row3 = kept[7] * (before - last)
            for k in range(levels):
                for at, add in ((0, row0), (1, row1), (tall - 2, row2), (tall - 1, row3)):
                    apply(t, k, h, at, add[k : k + 1, :])


def received(side_a, side_b, rows, even_lon):
    one, other = side_a[rows, :], side_b[rows, :]
    return jnp.where(even_lon, other, one), jnp.where(even_lon, one, other)


def add_rows(state, offset):
    def apply(t, k, h, at, add):
        spot = (t, k, h, slice(offset + at, offset + at + 1), slice(None))
        state[spot] = state[spot] + add

    return apply


def edge_kernel(
    got_a, got_b, sent, rows_a, rows_b, own, row_own, packed, index, before, c_in,
    c, next_side, next_rows_a, next_rows_b, correction,
):
    levels, tall = before.shape[1], own.shape[0]
    tiles = tall // SUB
    even_lon = parity("lon")

    def one_tile(r):
        rows = tile_rows(r)
        west, east = received(got_a, got_b, rows, even_lon)
        return side_correction(west, east, west, sent[rows, :], own[rows, :])

    def middle(r, carry):
        rows = tile_rows(r)
        found = one_tile(r)
        correction[rows, :] = found
        next_side[rows, :] = packed[rows, :] + found
        return carry

    lax.fori_loop(1, tiles - 1, middle, 0)
    row_corrections(before, PAD, rows_a, rows_b, rows_a, rows_b, row_own, index, tall, levels, add_rows(c, PAD))
    for r in (0, tiles - 1):
        rows = tile_rows(r)
        found = one_tile(r)
        correction[rows, :] = jnp.zeros((SUB, LANES), F32)
        fix_tile(c, r, found, levels)
        next_side[rows, :] = packed_edges(lambda t, k, h: c[t, k, h, tile_rows(r, PAD), :], levels)
    send_rows(c, next_rows_a, next_rows_b, levels, tall)


def fix_tile(c, r, found, levels):
    for t in range(TRACERS):
        for k in range(levels):
            new = add_sides(lambda h: c[t, k, h, tile_rows(r, PAD), :], found, t * levels + k)
            for h in range(2):
                c[t, k, h, tile_rows(r, PAD), :] = new[h]


def second_kernel(c_in, correction, terms, wet, mixing, c, out, south):
    levels, tall = wet.shape[0], wet.shape[2]
    tiles = tall // SUB
    for t in range(TRACERS):
        for k in range(levels):
            for h in range(2):
                south[t, k, h, 0:PAD, :] = jnp.zeros((PAD, LANES), F32)

    def body(r, carry):
        fix_tile(c, r + 1, correction[tile_rows(r + 1), :], levels)
        advance_tile(r, c, south, terms, wet, mixing, out, 0)
        return carry

    lax.fori_loop(0, tiles - 1, body, 0)
    advance_tile(tiles - 1, c, south, terms, wet, mixing, out, 0)


def last_kernel(
    got_a, got_b, sent, first_a, first_b, rows_a, rows_b, faces_a, faces_b, own, row_own, index, before, wet, c_in,
    fields, density, c, fields_out, density_out, sems,
):
    levels, tall = before.shape[1], own.shape[0]
    even_lon = parity("lon")
    row_corrections(before, PAD, rows_a, rows_b, faces_a, faces_b, row_own, index, tall, levels, add_rows(c, 0))

    def body(r, carry):
        rows = tile_rows(r)
        west, east = received(got_a, got_b, rows, even_lon)
        faces, _ = received(first_a, first_b, rows, even_lon)
        found = side_correction(west, east, faces, sent[rows, :], own[rows, :])
        for k in range(levels):
            new = [add_sides(lambda h: c[t, k, h, rows, :], found, t * levels + k) for t in range(TRACERS)]
            for h in range(2):
                for t in range(TRACERS):
                    fields_out[t, k, h, rows, :] = new[t][h]
                heat, salt = new[0][h], new[1][h]
                density_out[k, h, rows, :] = wet[k, h, rows, :] * (0.8 * salt - 0.2 * heat - 0.05 * heat * heat)
        return carry

    cuts = [0, 40, 80, 120, tall]
    copies = []
    for i, (lo, hi) in enumerate(zip(cuts[:-1], cuts[1:])):
        lax.fori_loop(lo // SUB, hi // SUB, body, 0)
        for h in range(2):
            cols = slice(h * LANES, (h + 1) * LANES)
            copies.append(
                pltpu.make_async_copy(
                    fields_out.at[:, :, h, lo:hi, :], fields.at[:, :, lo:hi, cols], sems.at[4 * i + h]
                )
            )
            copies.append(
                pltpu.make_async_copy(
                    density_out.at[:, h, lo:hi, :], density.at[:, lo:hi, cols], sems.at[4 * i + 2 + h]
                )
            )
        for one in copies[-4:]:
            one.start()
    for one in copies:
        one.wait()


def vmem(*shape, dtype=F32):
    return pltpu.VMEM(shape, dtype)


ON_CHIP = pl.BlockSpec(memory_space=pltpu.VMEM)
ANYWHERE = pl.BlockSpec(memory_space=pltpu.HBM)
SCALARS = pl.BlockSpec(memory_space=pltpu.SMEM)


def call(kernel, ins, out_shape, out_specs, scratch, cost, aliases=None):
    return pl.pallas_call(
        kernel,
        out_shape=out_shape,
        in_specs=ins,
        out_specs=out_specs,
        scratch_shapes=scratch,
        input_output_aliases=aliases or {},
        cost_estimate=pl.CostEstimate(flops=cost[0], bytes_accessed=cost[1], transcendentals=0),
        compiler_params=pltpu.CompilerParams(vmem_limit_bytes=VMEM_BYTES),
    )


def pairings(lats, lons):
    place = lambda a, o: (a % lats) * lons + o % lons
    by = {"lon_a": [], "lon_b": [], "lat_a": [], "lat_b": []}
    for a in range(lats):
        for o in range(lons):
            me = place(a, o)
            by["lon_a"].append((me, place(a, o ^ 1)))
            by["lon_b"].append((me, place(a, o + 1 if o % 2 else o - 1)))
            by["lat_a"].append((me, place(a ^ 1, o)))
            if a == lats - 1:
                other = place(a, lons - 1 - o)
            elif a == 0:
                other = place(a, o ^ 1)
            else:
                other = place(a + 1 if a % 2 else a - 1, o)
            by["lat_b"].append((me, other))
    return by


def on_device(pairs, tracers, east_faces, north_faces, land_mask, fold_partner, vert_mix):
    _, levels, tall, wide = tracers.shape
    assert wide == 2 * LANES and TRACERS * levels * 8 == LANES and tall % SUB == 0
    index = (fold_partner & (wide - 1)).reshape(1, wide)
    both = ("lat", "lon")
    swap = lambda x, name: lax.ppermute(x, both, pairs[name])
    tracers, east_faces, north_faces, land_mask = (
        pltpu.with_memory_space_constraint(x, pltpu.HBM) for x in (tracers, east_faces, north_faces, land_mask)
    )
    state = vmem(TRACERS, levels, 2, tall + 2 * PAD, LANES)
    side, rows3, rows2 = vmem(tall, LANES), vmem(6 * levels, wide), vmem(4 * levels, wide)
    faces = vmem(2, levels, 2, tall, LANES)
    level = vmem(levels, 2, tall, LANES)
    grid_bytes = tracers.size * 4

    c0, sent, rows_a, rows_b = call(
        start_kernel,
        [ANYWHERE] * 3,
        [state, side, rows3, rows3],
        [ON_CHIP] * 4,
        [vmem(2, levels, tall, LANES), vmem(2, levels, SUB, wide), pltpu.SemaphoreType.DMA((13,))],
        (1000000, 2 * grid_bytes),
    )(tracers, east_faces, north_faces)
    got_a, got_b = swap(sent, "lon_a"), swap(sent, "lon_b")
    got_rows_a, got_rows_b = swap(rows_a, "lat_a"), swap(rows_b, "lat_b")
    c1, packed, own, row_own, terms, wet, mixing = call(
        inner_kernel,
        [ON_CHIP, ANYWHERE, ANYWHERE, ANYWHERE, SCALARS],
        [state, side, side, vmem(8 * levels, wide), vmem(2, 3, levels, 2, tall, LANES), level,
         vmem(levels - 1, 2, tall, LANES)],
        [ON_CHIP] * 7,
        [faces, faces, vmem(levels, 2, tall, LANES, dtype=jnp.int32),
         vmem(TRACERS, levels, 2, tall + PAD, LANES), pltpu.SemaphoreType.DMA((24,))],
        (40000000, 4 * grid_bytes),
    )(c0, east_faces, north_faces, land_mask, vert_mix)
    c1, next_side, next_rows_a, next_rows_b, correction = call(
        edge_kernel,
        [ON_CHIP] * 11,
        [state, side, rows2, rows2, side],
        [ON_CHIP] * 5,
        [],
        (1000000, 1000000),
        {10: 0},
    )(got_a, got_b, sent, got_rows_a, got_rows_b, own, row_own, packed, index, c0, c1)
    new_a, new_b = swap(next_side, "lon_a"), swap(next_side, "lon_b")
    new_rows_a, new_rows_b = swap(next_rows_a, "lat_a"), swap(next_rows_b, "lat_b")
    c1, c2 = call(
        second_kernel,
        [ON_CHIP] * 5,
        [state, vmem(TRACERS, levels, 2, tall, LANES)],
        [ON_CHIP] * 2,
        [vmem(TRACERS, levels, 2, tall + PAD, LANES)],
        (40000000, 4 * grid_bytes),
        {0: 0},
    )(c1, correction, terms, wet, mixing)
    fields, density, _ = call(
        last_kernel,
        [ON_CHIP] * 15,
        [
            jax.ShapeDtypeStruct(tracers.shape, F32),
            jax.ShapeDtypeStruct(land_mask.shape, F32),
            vmem(TRACERS, levels, 2, tall, LANES),
        ],
        [ANYWHERE, ANYWHERE, ON_CHIP],
        [vmem(TRACERS, levels, 2, tall, LANES), level, pltpu.SemaphoreType.DMA((16,))],
        (4000000, 2 * grid_bytes),
        {14: 2},
    )(
        new_a, new_b, next_side, got_a, got_b, new_rows_a, new_rows_b, got_rows_a, got_rows_b,
        own, row_own, index, c1, wet, c2,
    )
    return fields, density


def solution(mesh):
    in_specs = (
        P(None, None, "lat", "lon"),
        P(None, None, "lat", "lon"),
        P(None, None, "lat", "lon"),
        P(None, "lat", "lon"),
        P("lon"),
        P(),
    )
    out_specs = (P(None, None, "lat", "lon"), P(None, "lat", "lon"))
    pairs = pairings(mesh.shape["lat"], mesh.shape["lon"])

    def body(*args):
        return on_device(pairs, *args)

    return jax.shard_map(body, mesh=mesh, in_specs=in_specs, out_specs=out_specs, check_vma=False)
```

```python
import jax
import jax.numpy as jnp
from jax import lax
from jax.experimental import pallas as pl
from jax.experimental.pallas import tpu as pltpu
from jax.sharding import PartitionSpec as P

F32 = jnp.float32
LANES = 128
SUB = 8
PAD = 8
TRACERS = 2
VMEM_BYTES = 14 * 1024 * 1024


def lane_ids():
    return lax.broadcasted_iota(jnp.int32, (SUB, LANES), 1)


def rolled(x, by):
    by = by % LANES
    return x if by == 0 else pltpu.roll(x, by, 1)


def face_terms(flow, spread):
    g = 0.125 * flow
    up = flow > 0.0
    g3 = 3.0 * g
    g6 = 6.0 * g
    return jnp.where(up, g6, g3) + spread, jnp.where(up, g3, g6) - spread, g, up


def tile_rows(index, offset=0):
    if isinstance(index, int):
        return pl.ds(index * SUB + offset, SUB)
    return pl.ds(pl.multiple_of(index * SUB, SUB) + offset, SUB)


def set_terms(r, east, north, mask, mix, terms, wet, mixing):
    levels = wet.shape[0]
    rows = tile_rows(r)
    for h in range(2):
        cells = [mask[k, h, rows, :].astype(F32) for k in range(levels)]
        for k in range(levels):
            wet[k, h, rows, :] = cells[k]
            if k + 1 < levels:
                mixing[k, h, rows, :] = mix[k] * cells[k] * cells[k + 1]
            for way, faces in enumerate((east, north)):
                a, b, g, _ = face_terms(faces[0, k, h, rows, :], faces[1, k, h, rows, :])
                for j, one in enumerate((a, b, g)):
                    terms[way, j, k, h, rows, :] = one


def advance_tile(r, c, south, terms, wet, mixing, out, out_pad):
    levels = wet.shape[0]
    lane = lane_ids()
    first, last, last2 = lane > 0, lane < LANES - 1, lane < LANES - 2
    rows = tile_rows(r)

    def cells(t, k, h, by=0):
        return c[t, k, h, tile_rows(r, PAD + by), :]

    for k in range(levels):
        for h in range(2):
            a, b, g = (terms[1, j, k, h, rows, :] for j in range(3))
            up = g > 0.0
            for t in range(TRACERS):
                further = jnp.where(up, cells(t, k, h, -1), cells(t, k, h, 2))
                face = a * cells(t, k, h) + b * cells(t, k, h, 1) - g * further
                south[t, k, h, tile_rows(r, PAD), :] = face
    below = [[None] * 2 for _ in range(TRACERS)]
    for k in range(levels):
        for t in range(TRACERS):
            c0 = [cells(t, k, h) for h in range(2)]
            plus1 = [rolled(x, -1) for x in c0]
            plus2 = [rolled(x, -2) for x in c0]
            minus1 = [rolled(x, 1) for x in c0]
            p1 = jnp.where(last, plus1[0], plus1[1]), jnp.where(last, plus1[1], 0.0)
            p2 = jnp.where(last2, plus2[0], plus2[1]), jnp.where(last2, plus2[1], 0.0)
            m1 = jnp.where(first, minus1[0], 0.0), jnp.where(first, minus1[1], minus1[0])
            flux = []
            for h in range(2):
                a, b, g = (terms[0, j, k, h, rows, :] for j in range(3))
                flux.append(a * c0[h] + b * p1[h] - g * jnp.where(g > 0.0, m1[h], p2[h]))
            shifted = [rolled(x, 1) for x in flux]
            west = jnp.where(first, shifted[0], 0.0), jnp.where(first, shifted[1], shifted[0])
            for h in range(2):
                change = west[h] - flux[h]
                change = change + (south[t, k, h, tile_rows(r, PAD - 1), :] - south[t, k, h, tile_rows(r, PAD), :])
                if k + 1 < levels:
                    vertical = mixing[k, h, rows, :] * (cells(t, k + 1, h) - c0[h])
                    change = change + vertical
                if k > 0:
                    change = change - below[t][h]
                if k + 1 < levels:
                    below[t][h] = vertical
                out[t, k, h, tile_rows(r, out_pad), :] = c0[h] + wet[k, h, rows, :] * change


class Step:
    def __init__(self, c, east_next, east_far, along, south, terms, wet, mixing, out, out_pad):
        self.c, self.east_next, self.east_far, self.along, self.south = c, east_next, east_far, along, south
        self.terms, self.wet, self.mixing, self.out, self.out_pad = terms, wet, mixing, out, out_pad
        self.levels = wet.shape[0]
        self.below = {}

    def cells(self, t, k, h, i, ahead, by=0):
        return self.c[t, k, h, tile_rows(i, PAD + ahead * SUB + by), :]

    def neighbours(self, i, ahead, k, t):
        lane = lane_ids()
        first, last, last2 = lane > 0, lane < LANES - 1, lane < LANES - 2
        rows = tile_rows(i, ahead * SUB)
        c0 = [self.cells(t, k, h, i, ahead) for h in range(2)]
        plus1 = [rolled(x, -1) for x in c0]
        plus2 = [rolled(x, -2) for x in c0]
        minus1 = [rolled(x, 1) for x in c0]
        p1 = jnp.where(last, plus1[0], plus1[1]), jnp.where(last, plus1[1], 0.0)
        p2 = jnp.where(last2, plus2[0], plus2[1]), jnp.where(last2, plus2[1], 0.0)
        m1 = jnp.where(first, minus1[0], 0.0), jnp.where(first, minus1[1], minus1[0])
        for h in range(2):
            self.east_next[t, k, h, rows, :] = p1[h]
            self.east_far[t, k, h, rows, :] = jnp.where(self.terms[0, 2, k, h, rows, :] > 0.0, m1[h], p2[h])

    def fluxes(self, i, ahead, k, t):
        first = lane_ids() > 0
        rows = tile_rows(i, ahead * SUB)
        flux = []
        for h in range(2):
            a, b, g = (self.terms[0, j, k, h, rows, :] for j in range(3))
            flux.append(
                a * self.cells(t, k, h, i, ahead)
                + b * self.east_next[t, k, h, rows, :]
                - g * self.east_far[t, k, h, rows, :]
            )
        shifted = [rolled(x, 1) for x in flux]
        west = jnp.where(first, shifted[0], 0.0), jnp.where(first, shifted[1], shifted[0])
        for h in range(2):
            self.along[t, k, h, rows, :] = west[h] - flux[h]
            a, b, g = (self.terms[1, j, k, h, rows, :] for j in range(3))
            further = jnp.where(g > 0.0, self.cells(t, k, h, i, ahead, -1), self.cells(t, k, h, i, ahead, 2))
            self.south[t, k, h, tile_rows(i, PAD + ahead * SUB), :] = (
                a * self.cells(t, k, h, i, ahead) + b * self.cells(t, k, h, i, ahead, 1) - g * further
            )

    def finish(self, i, ahead, k, t):
        rows = tile_rows(i, ahead * SUB)
        for h in range(2):
            c0 = self.cells(t, k, h, i, ahead)
            change = self.along[t, k, h, rows, :] + (
                self.south[t, k, h, tile_rows(i, PAD + ahead * SUB - 1), :]
                - self.south[t, k, h, tile_rows(i, PAD + ahead * SUB), :]
            )
            if k > 0:
                change = change - self.below[t, h]
            if k + 1 < self.levels:
                self.below[t, h] = self.mixing[k, h, rows, :] * (self.cells(t, k + 1, h, i, ahead) - c0)
                change = change + self.below[t, h]
            place = tile_rows(i, self.out_pad + ahead * SUB)
            self.out[t, k, h, place, :] = c0 + self.wet[k, h, rows, :] * change

    def turn(self, i, tiles, before=None, after=None):
        inside = lambda ahead: 0 <= i + ahead < tiles
        packs = after(i, -3) if after is not None and inside(-3) else None
        for k in range(self.levels):
            for t in range(TRACERS):
                if inside(-2):
                    self.finish(i, -2, k, t)
                if inside(-1):
                    self.fluxes(i, -1, k, t)
                if inside(0):
                    self.neighbours(i, 0, k, t)
                if before is not None and inside(1):
                    before(i, 1, k, t)
            if packs is not None:
                packs(k)


WINDOW = 5


def windows(i, refs, more):
    start = pl.multiple_of((i - 3) * SUB, SUB)
    seen = []
    for ref, rows in zip(refs, more):
        before = (slice(None),) * (len(ref.shape) - 2)
        seen.append(ref.at[before + (pl.ds(start, WINDOW * SUB + rows), slice(None))])
    return seen


def group(tl):
    lane = lane_ids()
    return lax.bitwise_and(lax.shift_right_logical(lane + 2, 3), LANES // SUB - 1) == tl


def slots():
    return lax.bitwise_and(lane_ids() + 2, 7) - 2


def packed_edges(get, levels, extra=None):
    lane = lane_ids()
    packed = jnp.zeros((SUB, LANES), F32)
    for t in range(TRACERS):
        for k in range(levels):
            tl = t * levels + k
            one = jnp.where(lane >= LANES - 2, get(t, k, 1), get(t, k, 0))
            if extra is not None:
                one = jnp.where(jnp.logical_and(lane >= 2, lane < 4), extra[k], one)
            packed = jnp.where(group(tl), rolled(one, 8 * tl), packed)
    return packed


def parity(axis):
    return lax.rem(lax.axis_index(axis), 2) == 0


def start_kernel(tracers, east, north, c, side, side_again, rows_a, rows_b, east_last, north_top, sems):
    levels, tall = tracers.shape[1], tracers.shape[2]
    cuts = [0, 40, 80, 120, tall]
    copies = []
    for i, (lo, hi) in enumerate(zip(cuts[:-1], cuts[1:])):
        group_of = []
        for h in range(2):
            group_of.append(
                pltpu.make_async_copy(
                    tracers.at[:, :, lo:hi, h * LANES : (h + 1) * LANES],
                    c.at[:, :, h, PAD + lo : PAD + hi, :],
                    sems.at[3 * i + h],
                )
            )
        group_of.append(
            pltpu.make_async_copy(
                east.at[:, :, lo:hi, LANES:], east_last.at[:, :, lo:hi, :], sems.at[3 * i + 2]
            )
        )
        copies.append(group_of)
    top_copy = pltpu.make_async_copy(north.at[:, :, tall - SUB :, :], north_top, sems.at[12])
    for group_of in copies:
        for one in group_of:
            one.start()
    top_copy.start()
    for t in range(TRACERS):
        for k in range(levels):
            for h in range(2):
                c[t, k, h, 0:PAD, :] = jnp.zeros((PAD, LANES), F32)
                c[t, k, h, PAD + tall :, :] = jnp.zeros((PAD, LANES), F32)
    lane = lane_ids()

    def pack(r, carry):
        rows = tile_rows(r)
        faces = []
        for k in range(levels):
            faces.append(
                jnp.where(lane == 2, rolled(east_last[0, k, rows, :], 3), rolled(east_last[1, k, rows, :], 4))
            )
        side[rows, :] = packed_edges(lambda t, k, h: c[t, k, h, tile_rows(r, PAD), :], levels, faces)
        side_again[rows, :] = side[rows, :]
        return carry

    for i, (lo, hi) in enumerate(zip(cuts[:-1], cuts[1:])):
        for one in copies[i]:
            one.wait()
        lax.fori_loop(lo // SUB, hi // SUB, pack, 0, unroll=True)
    top_copy.wait()
    send_rows(c, rows_a, rows_b, levels, tall)
    for comp in range(2):
        for k in range(levels):
            one_row = north_top[comp, k, SUB - 1 : SUB, :]
            at = 2 * TRACERS * levels + comp * levels + k
            rows_a[at : at + 1, :] = one_row
            rows_b[at : at + 1, :] = one_row


def send_rows(c, rows_a, rows_b, levels, tall):
    even_lat = parity("lat")
    for depth in range(2):
        top, bottom = PAD + tall - 1 - depth, PAD + depth
        at_a = jnp.where(even_lat, top, bottom)
        at_b = jnp.where(even_lat, bottom, top)
        for t in range(TRACERS):
            for k in range(levels):
                tl = (depth * TRACERS + t) * levels + k
                for h in range(2):
                    cols = slice(h * LANES, (h + 1) * LANES)
                    rows_a[tl : tl + 1, cols] = c[t, k, h, pl.ds(at_a, 1), :]
                    rows_b[tl : tl + 1, cols] = c[t, k, h, pl.ds(at_b, 1), :]


def inner_copies(pieces, east, north, mask, east_in, north_in, mask_in, sems):
    copies = []
    for i, (lo, hi) in enumerate(pieces):
        group_of = []
        for h in range(2):
            cols = slice(h * LANES, (h + 1) * LANES)
            for j, (src, dst) in enumerate(((east, east_in), (north, north_in))):
                group_of.append(
                    pltpu.make_async_copy(
                        src.at[:, :, lo:hi, cols], dst.at[:, :, h, lo:hi, :], sems.at[6 * i + 3 * h + j]
                    )
                )
            group_of.append(
                pltpu.make_async_copy(
                    mask.at[:, lo:hi, cols], mask_in.at[:, h, lo:hi, :], sems.at[6 * i + 3 * h + 2]
                )
            )
        copies.append(group_of)
    return copies


def clear(ref, rows):
    for t in range(TRACERS):
        for k in range(ref.shape[1]):
            for h in range(2):
                ref[t, k, h, rows, :] = jnp.zeros((PAD, LANES), F32)


def inner_tile(r, c, mix, out, packed, own, terms, wet, mixing, south, east_in, north_in, mask_in):
    levels = wet.shape[0]
    lane = lane_ids()
    rows = tile_rows(r)
    set_terms(r, east_in, north_in, mask_in, mix, terms, wet, mixing)
    advance_tile(r, c, south, terms, wet, mixing, out, PAD)
    packed[rows, :] = packed_edges(lambda t, k, h: out[t, k, h, tile_rows(r, PAD), :], levels)
    kept = jnp.zeros((SUB, LANES), F32)
    edge = lane >= LANES - 2
    for k in range(levels):
        one = jnp.where(edge, wet[k, 1, rows, :], wet[k, 0, rows, :])
        g = jnp.where(edge, terms[0, 2, k, 1, rows, :], terms[0, 2, k, 0, rows, :])
        some = jnp.where(lane == 5, rolled(terms[0, 1, k, 1, rows, :], 6), rolled(g, 4))
        one = jnp.where(jnp.logical_and(lane >= 2, lane < 6), some, one)
        kept = jnp.where(group(k), rolled(one, 8 * k), kept)
    own[rows, :] = jnp.where(jnp.logical_or(lane < LANES // 2 - 2, edge), kept, rolled(kept, LANES // 2))


FIRST_PIECES = ((0, 24), (24, 64))
REST_PIECES = ((64, 88), (88, 120), (120, 152))


def share(parts):
    place = lax.axis_index("lon") // 2
    amount = jnp.int32(0)
    for i, part in enumerate(parts):
        amount = jnp.where(place == i, part, amount)
    return amount


EARLY_TILES = (8, 5, 3, 2)
EARLY_TURNS = (10, 6, 3, 1)


def early_kernel(
    c, east, north, mask, mix, side_in, rows_in,
    out, packed, own, terms, wet, mixing, south, side, rows_b, east_in, north_in, mask_in, sems,
):
    count = share(EARLY_TILES)

    @pl.when(count > 0)
    def _():
        clear(south, slice(0, PAD))
        run_pieces(
            FIRST_PIECES, c, east, north, mask, mix, out, packed, own, terms, wet, mixing, south,
            east_in, north_in, mask_in, sems, count,
        )


def run_pieces(
    pieces, c, east, north, mask, mix, out, packed, own, terms, wet, mixing, south, east_in, north_in, mask_in, sems,
    count,
):
    copies = inner_copies(pieces, east, north, mask, east_in, north_in, mask_in, sems)

    def body(r, carry):
        inner_tile(r, c, mix, out, packed, own, terms, wet, mixing, south, east_in, north_in, mask_in)
        return carry

    for group_of in copies:
        for one in group_of:
            one.start()
    for (lo, hi), group_of in zip(pieces, copies):
        for one in group_of:
            one.wait()
        lax.fori_loop(lo // SUB, jnp.minimum(hi // SUB, count), body, 0)


def inner_kernel(
    c, east, north, mask, mix, out_in, packed_in, own_in, terms_in, wet_in, mixing_in, south_in,
    out, packed, own, terms, wet, mixing, south, row_own, east_in, north_in, mask_in, sems,
):
    levels, tall = wet.shape[0], wet.shape[2]
    done = share(EARLY_TILES)
    clear(out, slice(0, PAD))
    clear(out, slice(PAD + tall, PAD + tall + PAD))

    @pl.when(done == 0)
    def _():
        clear(south, slice(0, PAD))

    pieces = FIRST_PIECES + REST_PIECES
    copies = inner_copies(pieces, east, north, mask, east_in, north_in, mask_in, sems)

    def body(r, carry):
        inner_tile(r, c, mix, out, packed, own, terms, wet, mixing, south, east_in, north_in, mask_in)
        return carry

    for (lo, hi), group_of in zip(pieces, copies):

        @pl.when(done < hi // SUB)
        def _(group_of=group_of):
            for one in group_of:
                one.start()

    for (lo, hi), group_of in zip(pieces, copies):

        @pl.when(done < hi // SUB)
        def _(lo=lo, hi=hi, group_of=group_of):
            for one in group_of:
                one.wait()
            lax.fori_loop(jnp.maximum(lo // SUB, done), hi // SUB, body, 0)

    for k in range(levels):
        for h in range(2):
            cols = slice(h * LANES, (h + 1) * LANES)
            kept_rows = (
                terms[1, 2, k, h, 0:1, :],
                terms[1, 2, k, h, tall - 2 : tall - 1, :],
                terms[1, 2, k, h, tall - 1 : tall, :],
                terms[1, 1, k, h, tall - 1 : tall, :],
                wet[k, h, 0:1, :],
                wet[k, h, 1:2, :],
                wet[k, h, tall - 2 : tall - 1, :],
                wet[k, h, tall - 1 : tall, :],
            )
            for j, one in enumerate(kept_rows):
                row_own[j * levels + k : j * levels + k + 1, cols] = one


def side_correction(west, east, faces, mine, own):
    slot = slots()
    a, b, g, up = face_terms(rolled(faces, -2), rolled(faces, -3))
    near = rolled(west, 1)
    flux = a * near + b * mine - g * jnp.where(up, rolled(west, 2), rolled(mine, -1))
    mine_g = rolled(own, -4)
    first = jnp.maximum(mine_g, 0.0) * near
    beyond = jnp.minimum(mine_g, 0.0) * rolled(east, -2)
    last = rolled(beyond, 1) + rolled(own, -6) * rolled(east, -1)
    found = jnp.where(slot == 0, flux + first, -rolled(first, 1))
    found = jnp.where(slot < 0, beyond - jnp.where(slot == -1, last, 0.0), found)
    return jnp.where(slot < 2, own * found, 0.0)


def add_sides(get, correction, tl):
    lane = lane_ids()
    here = rolled(correction, -8 * tl)
    return get(0) + jnp.where(lane < 2, here, 0.0), get(1) + jnp.where(lane >= LANES - 2, here, 0.0)


def across_fold(x, index):
    picked = []
    for h in range(2):
        at = jnp.broadcast_to(index[:, h * LANES : (h + 1) * LANES], (SUB, LANES))
        at = lax.bitwise_and(at, 2 * LANES - 1)
        low = lax.bitwise_and(at, LANES - 1)
        parts = [jnp.take_along_axis(x[j], low, axis=1) for j in range(2)]
        picked.append(jnp.where(at < LANES, parts[0], parts[1]))
    return picked


def row_corrections(state, offset, rows_a, rows_b, faces_a, faces_b, row_own, index, tall, levels, apply):
    even_lat = parity("lat")
    lat = lax.axis_index("lat")
    at_top = lat == lax.axis_size("lat") - 1
    at_bottom = lat == 0
    for t in range(TRACERS):
        part = [slice((depth * TRACERS + t) * levels, (depth * TRACERS + t + 1) * levels) for depth in range(2)]
        north, south = [], []
        for depth in range(2):
            one, other = rows_a[part[depth], :], rows_b[part[depth], :]
            upper = jnp.where(even_lat, one, other)
            lower = jnp.where(even_lat, other, one)
            lower = jnp.where(at_bottom, 0.0, lower)
            upper = [upper[:, h * LANES : (h + 1) * LANES] for h in range(2)]
            folded = across_fold(upper, index)
            north.append([jnp.where(at_top, folded[h], upper[h]) for h in range(2)])
            south.append([lower[:, h * LANES : (h + 1) * LANES] for h in range(2)])
        for h in range(2):
            cols = slice(h * LANES, (h + 1) * LANES)
            base = 2 * TRACERS * levels
            faces = []
            for comp in range(2):
                span = slice(base + comp * levels, base + (comp + 1) * levels)
                one = jnp.where(even_lat, faces_b[span, cols], faces_a[span, cols])
                faces.append(jnp.where(at_bottom, 0.0, one))
            kept = [row_own[j * levels : (j + 1) * levels, cols] for j in range(8)]
            bottom = [
                jnp.concatenate([state[t, k, h, offset + j : offset + j + 1, :] for k in range(levels)], axis=0)
                for j in range(2)
            ]
            a, b, g, up = face_terms(faces[0], faces[1])
            flux = a * south[0][h] + b * bottom[0] - g * jnp.where(up, south[1][h], bottom[1])
            first = jnp.maximum(kept[0], 0.0) * south[0][h]
            row0 = kept[4] * (flux + first)
            row1 = -(kept[5] * first)
            last = kept[3] * north[0][h] - jnp.minimum(kept[2], 0.0) * north[1][h]
            before = -(jnp.minimum(kept[1], 0.0) * north[0][h])
            row2 = -(kept[6] * before)
            row3 = kept[7] * (before - last)
            for k in range(levels):
                for at, add in ((0, row0), (1, row1), (tall - 2, row2), (tall - 1, row3)):
                    apply(t, k, h, at, add[k : k + 1, :])


def received(side_a, side_b, rows, even_lon):
    one, other = side_a[rows, :], side_b[rows, :]
    return jnp.where(even_lon, other, one), jnp.where(even_lon, one, other)


def add_rows(state, offset):
    def apply(t, k, h, at, add):
        spot = (t, k, h, slice(offset + at, offset + at + 1), slice(None))
        state[spot] = state[spot] + add

    return apply


def edge_kernel(
    got_a, got_b, sent, rows_a, rows_b, own, row_own, packed, index, before, c_in,
    c, next_side, next_side_again, next_rows_a, next_rows_b, correction,
):
    levels, tall = before.shape[1], own.shape[0]
    tiles = tall // SUB
    even_lon = parity("lon")

    def one_tile(r):
        rows = tile_rows(r)
        west, east = received(got_a, got_b, rows, even_lon)
        return side_correction(west, east, west, sent[rows, :], own[rows, :])

    def middle(r, carry):
        rows = tile_rows(r)
        found = one_tile(r)
        correction[rows, :] = found
        next_side[rows, :] = packed[rows, :] + found
        next_side_again[rows, :] = packed[rows, :] + found
        return carry

    lax.fori_loop(1, tiles - 1, middle, 0, unroll=True)
    row_corrections(before, PAD, rows_a, rows_b, rows_a, rows_b, row_own, index, tall, levels, add_rows(c, PAD))
    for r in (0, tiles - 1):
        rows = tile_rows(r)
        found = one_tile(r)
        correction[rows, :] = jnp.zeros((SUB, LANES), F32)
        fix_tile(c, r, found, levels)
        sides = packed_edges(lambda t, k, h: c[t, k, h, tile_rows(r, PAD), :], levels)
        next_side[rows, :] = sides
        next_side_again[rows, :] = sides
    send_rows(c, next_rows_a, next_rows_b, levels, tall)


def fix_tile(c, r, found, levels):
    for t in range(TRACERS):
        for k in range(levels):
            new = add_sides(lambda h: c[t, k, h, tile_rows(r, PAD), :], found, t * levels + k)
            for h in range(2):
                c[t, k, h, tile_rows(r, PAD), :] = new[h]


def second_turns(c, correction, terms, wet, mixing, out, south, east_next, east_far, along):
    levels, tall = wet.shape[0], wet.shape[2]
    tiles = tall // SUB
    whole = (c, east_next, east_far, along, south, terms, wet, mixing, out, correction)
    more = (2 * PAD, 0, 0, 0, PAD, 0, 0, 0, 0, 0)

    def turn(i, count, refs):
        c, east_next, east_far, along, south, terms, wet, mixing, out, correction = refs
        step = Step(c, east_next, east_far, along, south, terms, wet, mixing, out, 0)

        def ready(i, ahead, k, t):
            rows = tile_rows(i, PAD + ahead * SUB)
            found = correction[tile_rows(i, ahead * SUB), :]
            new = add_sides(lambda h: c[t, k, h, rows, :], found, t * levels + k)
            for h in range(2):
                c[t, k, h, rows, :] = new[h]

        step.turn(i, count, ready)

    def begin():
        for t in range(TRACERS):
            for k in range(levels):
                for h in range(2):
                    south[t, k, h, 0:PAD, :] = jnp.zeros((PAD, LANES), F32)
        for i in range(-1, FIRST_TURN):
            turn(i, tiles, whole)

    def middle(lo, hi):
        def body(i, carry):
            turn(3, WINDOW, windows(i, whole, more))
            return carry

        lax.fori_loop(lo, hi, body, 0)

    def end():
        for i in range(tiles - 1, tiles + 2):
            turn(i, tiles, whole)

    return begin, middle, end


FIRST_TURN = 3


def second_early_kernel(
    c_in, side_in, side_again_in, rows_a_in, rows_b_in, correction, terms, wet, mixing,
    c, side, side_again, rows_a, rows_b, out, south, east_next, east_far, along,
):
    count = share(EARLY_TURNS)
    begin, middle, _ = second_turns(c, correction, terms, wet, mixing, out, south, east_next, east_far, along)

    @pl.when(count > 0)
    def _():
        begin()
        middle(FIRST_TURN, FIRST_TURN + count)


def second_kernel(
    c_in, out_in, south_in, east_next_in, east_far_in, along_in, correction, terms, wet, mixing,
    c, out, south, east_next, east_far, along,
):
    count = share(EARLY_TURNS)
    begin, middle, end = second_turns(c, correction, terms, wet, mixing, out, south, east_next, east_far, along)

    @pl.when(count == 0)
    def _():
        begin()

    middle(FIRST_TURN + count, wet.shape[2] // SUB - 1)
    end()


def last_kernel(
    got_a, got_b, sent, first_a, first_b, rows_a, rows_b, faces_a, faces_b, own, row_own, index, before, wet, c_in,
    fields, density, c, fields_out, density_out, sems,
):
    levels, tall = before.shape[1], own.shape[0]
    even_lon = parity("lon")
    row_corrections(before, PAD, rows_a, rows_b, faces_a, faces_b, row_own, index, tall, levels, add_rows(c, 0))

    def body(r, carry):
        rows = tile_rows(r)
        west, east = received(got_a, got_b, rows, even_lon)
        faces, _ = received(first_a, first_b, rows, even_lon)
        found = side_correction(west, east, faces, sent[rows, :], own[rows, :])
        for k in range(levels):
            new = [add_sides(lambda h: c[t, k, h, rows, :], found, t * levels + k) for t in range(TRACERS)]
            for h in range(2):
                for t in range(TRACERS):
                    fields_out[t, k, h, rows, :] = new[t][h]
                heat, salt = new[0][h], new[1][h]
                density_out[k, h, rows, :] = wet[k, h, rows, :] * (0.8 * salt - 0.2 * heat - 0.05 * heat * heat)
        return carry

    cuts = [0, 40, 80, 120, tall]
    copies = []
    for i, (lo, hi) in enumerate(zip(cuts[:-1], cuts[1:])):
        lax.fori_loop(lo // SUB, hi // SUB, body, 0, unroll=True)
        for h in range(2):
            cols = slice(h * LANES, (h + 1) * LANES)
            copies.append(
                pltpu.make_async_copy(
                    fields_out.at[:, :, h, lo:hi, :], fields.at[:, :, lo:hi, cols], sems.at[4 * i + h]
                )
            )
            copies.append(
                pltpu.make_async_copy(
                    density_out.at[:, h, lo:hi, :], density.at[:, lo:hi, cols], sems.at[4 * i + 2 + h]
                )
            )
        for one in copies[-4:]:
            one.start()
    for one in copies:
        one.wait()


def vmem(*shape, dtype=F32):
    return pltpu.VMEM(shape, dtype)


ON_CHIP = pl.BlockSpec(memory_space=pltpu.VMEM)
ANYWHERE = pl.BlockSpec(memory_space=pltpu.HBM)
SCALARS = pl.BlockSpec(memory_space=pltpu.SMEM)


def call(kernel, ins, out_shape, out_specs, scratch, cost, aliases=None):
    return pl.pallas_call(
        kernel,
        out_shape=out_shape,
        in_specs=ins,
        out_specs=out_specs,
        scratch_shapes=scratch,
        input_output_aliases=aliases or {},
        cost_estimate=pl.CostEstimate(flops=cost[0], bytes_accessed=cost[1], transcendentals=0),
        compiler_params=pltpu.CompilerParams(vmem_limit_bytes=VMEM_BYTES),
    )


def pairings(lats, lons):
    place = lambda a, o: (a % lats) * lons + o % lons
    by = {"lon_a": [], "lon_b": [], "lat_a": [], "lat_b": []}
    for a in range(lats):
        for o in range(lons):
            me = place(a, o)
            by["lon_a"].append((me, place(a, o ^ 1)))
            by["lon_b"].append((me, place(a, o + 1 if o % 2 else o - 1)))
            by["lat_a"].append((me, place(a ^ 1, o)))
            if a == lats - 1:
                other = place(a, lons - 1 - o)
            elif a == 0:
                other = place(a, o ^ 1)
            else:
                other = place(a + 1 if a % 2 else a - 1, o)
            by["lat_b"].append((me, other))
    return by


def on_device(pairs, tracers, east_faces, north_faces, land_mask, fold_partner, vert_mix):
    _, levels, tall, wide = tracers.shape
    assert wide == 2 * LANES and TRACERS * levels * 8 == LANES and tall % SUB == 0
    index = fold_partner.reshape(1, wide)
    both = ("lat", "lon")
    swap = lambda x, name: lax.ppermute(x, both, pairs[name])
    tracers, east_faces, north_faces, land_mask = (
        pltpu.with_memory_space_constraint(x, pltpu.HBM) for x in (tracers, east_faces, north_faces, land_mask)
    )
    state = vmem(TRACERS, levels, 2, tall + 2 * PAD, LANES)
    side, rows3, rows2 = vmem(tall, LANES), vmem(6 * levels, wide), vmem(4 * levels, wide)
    faces = vmem(2, levels, 2, tall, LANES)
    level = vmem(levels, 2, tall, LANES)
    grid = vmem(TRACERS, levels, 2, tall, LANES)
    grid_bytes = tracers.size * 4

    c0, sent, sent_again, rows_a, rows_b = call(
        start_kernel,
        [ANYWHERE] * 3,
        [state, side, side, rows3, rows3],
        [ON_CHIP] * 5,
        [vmem(2, levels, tall, LANES), vmem(2, levels, SUB, wide), pltpu.SemaphoreType.DMA((13,))],
        (1000000, 2 * grid_bytes),
    )(tracers, east_faces, north_faces)
    got_a, got_rows_a = swap(sent, "lon_a"), swap(rows_a, "lat_a")
    assert REST_PIECES[-1][1] == tall
    shared = [state, side, side, vmem(2, 3, levels, 2, tall, LANES), level, vmem(levels - 1, 2, tall, LANES),
              vmem(TRACERS, levels, 2, tall + PAD, LANES)]
    early_rows = FIRST_PIECES[-1][1]
    *state_so_far, sent_again, rows_b = call(
        early_kernel,
        [ON_CHIP, ANYWHERE, ANYWHERE, ANYWHERE, SCALARS, ON_CHIP, ON_CHIP],
        shared + [side, rows3],
        [ON_CHIP] * 9,
        [vmem(2, levels, 2, early_rows, LANES)] * 2
        + [vmem(levels, 2, early_rows, LANES, dtype=jnp.int32), pltpu.SemaphoreType.DMA((12,))],
        (10000000, grid_bytes),
        {5: 7, 6: 8},
    )(c0, east_faces, north_faces, land_mask, vert_mix, sent_again, rows_b)
    got_b, got_rows_b = swap(sent_again, "lon_b"), swap(rows_b, "lat_b")
    c1, packed, own, terms, wet, mixing, _, row_own = call(
        inner_kernel,
        [ON_CHIP, ANYWHERE, ANYWHERE, ANYWHERE, SCALARS] + [ON_CHIP] * 7,
        shared + [vmem(8 * levels, wide)],
        [ON_CHIP] * 8,
        [faces, faces, vmem(levels, 2, tall, LANES, dtype=jnp.int32), pltpu.SemaphoreType.DMA((30,))],
        (40000000, 4 * grid_bytes),
        {5 + j: j for j in range(7)},
    )(c0, east_faces, north_faces, land_mask, vert_mix, *state_so_far)
    c1, next_side, next_again, next_rows_a, next_rows_b, correction = call(
        edge_kernel,
        [ON_CHIP] * 11,
        [state, side, side, rows2, rows2, side],
        [ON_CHIP] * 6,
        [],
        (1000000, 1000000),
        {10: 0},
    )(got_a, got_b, sent, got_rows_a, got_rows_b, own, row_own, packed, index, c0, c1)
    kept = [grid, vmem(TRACERS, levels, 2, tall + PAD, LANES), grid, grid, grid]
    c1, sent_side, sent_side_again, next_rows_a, next_rows_b, *kept_so_far = call(
        second_early_kernel,
        [ON_CHIP] * 9,
        [state, side, side, rows2, rows2] + kept,
        [ON_CHIP] * 10,
        [],
        (10000000, grid_bytes),
        {j: j for j in range(5)},
    )(c1, next_side, next_again, next_rows_a, next_rows_b, correction, terms, wet, mixing)
    new_a, new_b = swap(sent_side, "lon_a"), swap(sent_side_again, "lon_b")
    new_rows_a, new_rows_b = swap(next_rows_a, "lat_a"), swap(next_rows_b, "lat_b")
    c1, c2, *_ = call(
        second_kernel,
        [ON_CHIP] * 10,
        [state] + kept,
        [ON_CHIP] * 6,
        [],
        (40000000, 4 * grid_bytes),
        {j: j for j in range(6)},
    )(c1, *kept_so_far, correction, terms, wet, mixing)
    fields, density, _ = call(
        last_kernel,
        [ON_CHIP] * 15,
        [
            jax.ShapeDtypeStruct(tracers.shape, F32),
            jax.ShapeDtypeStruct(land_mask.shape, F32),
            vmem(TRACERS, levels, 2, tall, LANES),
        ],
        [ANYWHERE, ANYWHERE, ON_CHIP],
        [vmem(TRACERS, levels, 2, tall, LANES), level, pltpu.SemaphoreType.DMA((16,))],
        (4000000, 2 * grid_bytes),
        {14: 2},
    )(
        new_a, new_b, sent_side, got_a, got_b, new_rows_a, new_rows_b, got_rows_a, got_rows_b,
        own, row_own, index, c1, wet, c2,
    )
    return fields, density


def solution(mesh):
    in_specs = (
        P(None, None, "lat", "lon"),
        P(None, None, "lat", "lon"),
        P(None, None, "lat", "lon"),
        P(None, "lat", "lon"),
        P("lon"),
        P(),
    )
    out_specs = (P(None, None, "lat", "lon"), P(None, "lat", "lon"))
    pairs = pairings(mesh.shape["lat"], mesh.shape["lon"])

    def body(*args):
        return on_device(pairs, *args)

    return jax.shard_map(body, mesh=mesh, in_specs=in_specs, out_specs=out_specs, check_vma=False)
```

```python
import jax
import jax.numpy as jnp
from jax import lax
from jax.experimental import pallas as pl
from jax.experimental.pallas import tpu as pltpu
from jax.sharding import PartitionSpec as P

F32 = jnp.float32
LANES = 128
SUB = 8
PAD = 8
TRACERS = 2
VMEM_BYTES = 14 * 1024 * 1024


def lane_ids():
    return lax.broadcasted_iota(jnp.int32, (SUB, LANES), 1)


def rolled(x, by):
    by = by % LANES
    return x if by == 0 else pltpu.roll(x, by, 1)


def face_terms(flow, spread):
    g = 0.125 * flow
    up = flow > 0.0
    g3 = 3.0 * g
    g6 = 6.0 * g
    return jnp.where(up, g6, g3) + spread, jnp.where(up, g3, g6) - spread, g, up


def tile_rows(index, offset=0):
    if isinstance(index, int):
        return pl.ds(index * SUB + offset, SUB)
    return pl.ds(pl.multiple_of(index * SUB, SUB) + offset, SUB)


def set_terms(r, east, north, mask, mix, terms, wet, mixing):
    levels = wet.shape[0]
    rows = tile_rows(r)
    for h in range(2):
        cells = [mask(k, h, rows).astype(F32) for k in range(levels)]
        for k in range(levels):
            wet[k, h, rows, :] = cells[k]
            if k + 1 < levels:
                mixing[k, h, rows, :] = mix[k] * cells[k] * cells[k + 1]
            for way, faces in enumerate((east, north)):
                a, b, g, _ = face_terms(faces(0, k, h, rows), faces(1, k, h, rows))
                for j, one in enumerate((a, b, g)):
                    terms[way, j, k, h, rows, :] = one


def halved(ref):
    return lambda *at: ref[at + (slice(None),)]


def whole(ref):
    return lambda *at: ref[at[:-2] + (at[-1], slice(at[-2] * LANES, (at[-2] + 1) * LANES))]


def advance_tile(r, c, south, terms, wet, mixing, out, out_pad):
    levels = wet.shape[0]
    lane = lane_ids()
    first, last, last2 = lane > 0, lane < LANES - 1, lane < LANES - 2
    rows = tile_rows(r)

    def cells(t, k, h, by=0):
        return c[t, k, h, tile_rows(r, PAD + by), :]

    for k in range(levels):
        for h in range(2):
            a, b, g = (terms[1, j, k, h, rows, :] for j in range(3))
            up = g > 0.0
            for t in range(TRACERS):
                further = jnp.where(up, cells(t, k, h, -1), cells(t, k, h, 2))
                face = a * cells(t, k, h) + b * cells(t, k, h, 1) - g * further
                south[t, k, h, tile_rows(r, PAD), :] = face
    below = [[None] * 2 for _ in range(TRACERS)]
    for k in range(levels):
        for t in range(TRACERS):
            c0 = [cells(t, k, h) for h in range(2)]
            plus1 = [rolled(x, -1) for x in c0]
            plus2 = [rolled(x, -2) for x in c0]
            minus1 = [rolled(x, 1) for x in c0]
            p1 = jnp.where(last, plus1[0], plus1[1]), jnp.where(last, plus1[1], 0.0)
            p2 = jnp.where(last2, plus2[0], plus2[1]), jnp.where(last2, plus2[1], 0.0)
            m1 = jnp.where(first, minus1[0], 0.0), jnp.where(first, minus1[1], minus1[0])
            flux = []
            for h in range(2):
                a, b, g = (terms[0, j, k, h, rows, :] for j in range(3))
                flux.append(a * c0[h] + b * p1[h] - g * jnp.where(g > 0.0, m1[h], p2[h]))
            shifted = [rolled(x, 1) for x in flux]
            west = jnp.where(first, shifted[0], 0.0), jnp.where(first, shifted[1], shifted[0])
            for h in range(2):
                change = west[h] - flux[h]
                change = change + (south[t, k, h, tile_rows(r, PAD - 1), :] - south[t, k, h, tile_rows(r, PAD), :])
                if k + 1 < levels:
                    vertical = mixing[k, h, rows, :] * (cells(t, k + 1, h) - c0[h])
                    change = change + vertical
                if k > 0:
                    change = change - below[t][h]
                if k + 1 < levels:
                    below[t][h] = vertical
                out[t, k, h, tile_rows(r, out_pad), :] = c0[h] + wet[k, h, rows, :] * change


class Step:
    def __init__(self, c, east_next, east_far, along, south, terms, wet, mixing, out, out_pad):
        self.c, self.east_next, self.east_far, self.along, self.south = c, east_next, east_far, along, south
        self.terms, self.wet, self.mixing, self.out, self.out_pad = terms, wet, mixing, out, out_pad
        self.levels = wet.shape[0]
        self.below = {}

    def cells(self, t, k, h, i, ahead, by=0):
        return self.c[t, k, h, tile_rows(i, PAD + ahead * SUB + by), :]

    def neighbours(self, i, ahead, k, t):
        lane = lane_ids()
        first, last, last2 = lane > 0, lane < LANES - 1, lane < LANES - 2
        rows = tile_rows(i, ahead * SUB)
        c0 = [self.cells(t, k, h, i, ahead) for h in range(2)]
        plus1 = [rolled(x, -1) for x in c0]
        plus2 = [rolled(x, -2) for x in c0]
        minus1 = [rolled(x, 1) for x in c0]
        p1 = jnp.where(last, plus1[0], plus1[1]), jnp.where(last, plus1[1], 0.0)
        p2 = jnp.where(last2, plus2[0], plus2[1]), jnp.where(last2, plus2[1], 0.0)
        m1 = jnp.where(first, minus1[0], 0.0), jnp.where(first, minus1[1], minus1[0])
        for h in range(2):
            self.east_next[t, k, h, rows, :] = p1[h]
            self.east_far[t, k, h, rows, :] = jnp.where(self.terms[0, 2, k, h, rows, :] > 0.0, m1[h], p2[h])

    def fluxes(self, i, ahead, k, t):
        first = lane_ids() > 0
        rows = tile_rows(i, ahead * SUB)
        flux = []
        for h in range(2):
            a, b, g = (self.terms[0, j, k, h, rows, :] for j in range(3))
            flux.append(
                a * self.cells(t, k, h, i, ahead)
                + b * self.east_next[t, k, h, rows, :]
                - g * self.east_far[t, k, h, rows, :]
            )
        shifted = [rolled(x, 1) for x in flux]
        west = jnp.where(first, shifted[0], 0.0), jnp.where(first, shifted[1], shifted[0])
        for h in range(2):
            self.along[t, k, h, rows, :] = west[h] - flux[h]
            a, b, g = (self.terms[1, j, k, h, rows, :] for j in range(3))
            further = jnp.where(g > 0.0, self.cells(t, k, h, i, ahead, -1), self.cells(t, k, h, i, ahead, 2))
            self.south[t, k, h, tile_rows(i, PAD + ahead * SUB), :] = (
                a * self.cells(t, k, h, i, ahead) + b * self.cells(t, k, h, i, ahead, 1) - g * further
            )

    def finish(self, i, ahead, k, t):
        rows = tile_rows(i, ahead * SUB)
        for h in range(2):
            c0 = self.cells(t, k, h, i, ahead)
            change = self.along[t, k, h, rows, :] + (
                self.south[t, k, h, tile_rows(i, PAD + ahead * SUB - 1), :]
                - self.south[t, k, h, tile_rows(i, PAD + ahead * SUB), :]
            )
            if k > 0:
                change = change - self.below[t, h]
            if k + 1 < self.levels:
                self.below[t, h] = self.mixing[k, h, rows, :] * (self.cells(t, k + 1, h, i, ahead) - c0)
                change = change + self.below[t, h]
            place = tile_rows(i, self.out_pad + ahead * SUB)
            self.out[t, k, h, place, :] = c0 + self.wet[k, h, rows, :] * change

    def turn(self, i, tiles, before=None, after=None):
        inside = lambda ahead: 0 <= i + ahead < tiles
        packs = after(i, -3) if after is not None and inside(-3) else None
        for k in range(self.levels):
            for t in range(TRACERS):
                if inside(-2):
                    self.finish(i, -2, k, t)
                if inside(-1):
                    self.fluxes(i, -1, k, t)
                if inside(0):
                    self.neighbours(i, 0, k, t)
                if before is not None and inside(1):
                    before(i, 1, k, t)
            if packs is not None:
                packs(k)


WINDOW = 5


def windows(i, refs, more):
    start = pl.multiple_of((i - 3) * SUB, SUB)
    seen = []
    for ref, rows in zip(refs, more):
        before = (slice(None),) * (len(ref.shape) - 2)
        seen.append(ref.at[before + (pl.ds(start, WINDOW * SUB + rows), slice(None))])
    return seen


def group(tl):
    lane = lane_ids()
    return lax.bitwise_and(lax.shift_right_logical(lane + 2, 3), LANES // SUB - 1) == tl


def slots():
    return lax.bitwise_and(lane_ids() + 2, 7) - 2


def packed_edges(get, levels, extra=None):
    lane = lane_ids()
    packed = jnp.zeros((SUB, LANES), F32)
    for t in range(TRACERS):
        for k in range(levels):
            tl = t * levels + k
            one = jnp.where(lane >= LANES - 2, get(t, k, 1), get(t, k, 0))
            if extra is not None:
                one = jnp.where(jnp.logical_and(lane >= 2, lane < 4), extra[k], one)
            packed = jnp.where(group(tl), rolled(one, 8 * tl), packed)
    return packed


def parity(axis):
    return lax.rem(lax.axis_index(axis), 2) == 0


def start_kernel(tracers, east, north, c, side, side_again, rows_a, rows_b, east_last, north_top, sems):
    levels, tall = tracers.shape[1], tracers.shape[2]
    cuts = [0, 40, 80, 120, tall]
    copies = []
    for i, (lo, hi) in enumerate(zip(cuts[:-1], cuts[1:])):
        group_of = []
        for h in range(2):
            group_of.append(
                pltpu.make_async_copy(
                    tracers.at[:, :, lo:hi, h * LANES : (h + 1) * LANES],
                    c.at[:, :, h, PAD + lo : PAD + hi, :],
                    sems.at[3 * i + h],
                )
            )
        group_of.append(
            pltpu.make_async_copy(
                east.at[:, :, lo:hi, LANES:], east_last.at[:, :, lo:hi, :], sems.at[3 * i + 2]
            )
        )
        copies.append(group_of)
    top_copy = pltpu.make_async_copy(north.at[:, :, tall - SUB :, :], north_top, sems.at[12])
    for group_of in copies:
        for one in group_of:
            one.start()
    top_copy.start()
    for t in range(TRACERS):
        for k in range(levels):
            for h in range(2):
                c[t, k, h, 0:PAD, :] = jnp.zeros((PAD, LANES), F32)
                c[t, k, h, PAD + tall :, :] = jnp.zeros((PAD, LANES), F32)
    lane = lane_ids()

    def pack(r, carry):
        rows = tile_rows(r)
        faces = []
        for k in range(levels):
            faces.append(
                jnp.where(lane == 2, rolled(east_last[0, k, rows, :], 3), rolled(east_last[1, k, rows, :], 4))
            )
        side[rows, :] = packed_edges(lambda t, k, h: c[t, k, h, tile_rows(r, PAD), :], levels, faces)
        side_again[rows, :] = side[rows, :]
        return carry

    for i, (lo, hi) in enumerate(zip(cuts[:-1], cuts[1:])):
        for one in copies[i]:
            one.wait()
        lax.fori_loop(lo // SUB, hi // SUB, pack, 0, unroll=True)
    top_copy.wait()
    send_rows(c, rows_a, rows_b, levels, tall)
    for comp in range(2):
        for k in range(levels):
            one_row = north_top[comp, k, SUB - 1 : SUB, :]
            at = 2 * TRACERS * levels + comp * levels + k
            rows_a[at : at + 1, :] = one_row
            rows_b[at : at + 1, :] = one_row


def send_rows(c, rows_a, rows_b, levels, tall):
    even_lat = parity("lat")
    for depth in range(2):
        top, bottom = PAD + tall - 1 - depth, PAD + depth
        at_a = jnp.where(even_lat, top, bottom)
        at_b = jnp.where(even_lat, bottom, top)
        for t in range(TRACERS):
            for k in range(levels):
                tl = (depth * TRACERS + t) * levels + k
                for h in range(2):
                    cols = slice(h * LANES, (h + 1) * LANES)
                    rows_a[tl : tl + 1, cols] = c[t, k, h, pl.ds(at_a, 1), :]
                    rows_b[tl : tl + 1, cols] = c[t, k, h, pl.ds(at_b, 1), :]


def inner_copies(pieces, east, north, mask, east_in, north_in, mask_in, sems):
    copies = []
    for i, (lo, hi) in enumerate(pieces):
        group_of = []
        for h in range(2):
            cols = slice(h * LANES, (h + 1) * LANES)
            for j, (src, dst) in enumerate(((east, east_in), (north, north_in))):
                group_of.append(
                    pltpu.make_async_copy(
                        src.at[:, :, lo:hi, cols], dst.at[:, :, h, lo:hi, :], sems.at[6 * i + 3 * h + j]
                    )
                )
            group_of.append(
                pltpu.make_async_copy(
                    mask.at[:, lo:hi, cols], mask_in.at[:, h, lo:hi, :], sems.at[6 * i + 3 * h + 2]
                )
            )
        copies.append(group_of)
    return copies


def clear(ref, rows):
    for t in range(TRACERS):
        for k in range(ref.shape[1]):
            for h in range(2):
                ref[t, k, h, rows, :] = jnp.zeros((PAD, LANES), F32)


def inner_tile(r, c, mix, out, packed, own, terms, wet, mixing, south, east_in, north_in, mask_in):
    levels = wet.shape[0]
    lane = lane_ids()
    rows = tile_rows(r)
    set_terms(r, east_in, north_in, mask_in, mix, terms, wet, mixing)
    advance_tile(r, c, south, terms, wet, mixing, out, PAD)
    packed[rows, :] = packed_edges(lambda t, k, h: out[t, k, h, tile_rows(r, PAD), :], levels)
    kept = jnp.zeros((SUB, LANES), F32)
    edge = lane >= LANES - 2
    for k in range(levels):
        one = jnp.where(edge, wet[k, 1, rows, :], wet[k, 0, rows, :])
        g = jnp.where(edge, terms[0, 2, k, 1, rows, :], terms[0, 2, k, 0, rows, :])
        some = jnp.where(lane == 5, rolled(terms[0, 1, k, 1, rows, :], 6), rolled(g, 4))
        one = jnp.where(jnp.logical_and(lane >= 2, lane < 6), some, one)
        kept = jnp.where(group(k), rolled(one, 8 * k), kept)
    own[rows, :] = jnp.where(jnp.logical_or(lane < LANES // 2 - 2, edge), kept, rolled(kept, LANES // 2))


FIRST_PIECES = ((0, 24), (24, 64))
REST_PIECES = ((64, 88), (88, 120), (120, 152))


def share(parts):
    place = lax.axis_index("lon") // 2
    amount = jnp.int32(0)
    for i, part in enumerate(parts):
        amount = jnp.where(place == i, part, amount)
    return amount


EARLY_TILES = (8, 5, 3, 2)
EARLY_TURNS = (10, 6, 3, 1)


def early_kernel(
    c, east, north, mask, mix, side_in, rows_in,
    out, packed, own, terms, wet, mixing, south, side, rows_b, east_in, north_in, mask_in, sems,
):
    count = share(EARLY_TILES)

    @pl.when(count > 0)
    def _():
        clear(south, slice(0, PAD))
        run_pieces(
            FIRST_PIECES, c, east, north, mask, mix, out, packed, own, terms, wet, mixing, south,
            east_in, north_in, mask_in, sems, count,
        )


def run_pieces(
    pieces, c, east, north, mask, mix, out, packed, own, terms, wet, mixing, south, east_in, north_in, mask_in, sems,
    count,
):
    copies = inner_copies(pieces, east, north, mask, east_in, north_in, mask_in, sems)

    def body(r, carry):
        faces = halved(east_in), halved(north_in), halved(mask_in)
        inner_tile(r, c, mix, out, packed, own, terms, wet, mixing, south, *faces)
        return carry

    for group_of in copies:
        for one in group_of:
            one.start()
    for (lo, hi), group_of in zip(pieces, copies):
        for one in group_of:
            one.wait()
        lax.fori_loop(lo // SUB, jnp.minimum(hi // SUB, count), body, 0)


def inner_kernel(
    c, east, north, mask, mix, out_in, packed_in, own_in, terms_in, wet_in, mixing_in, south_in,
    out, packed, own, terms, wet, mixing, south, row_own,
):
    levels, tall = wet.shape[0], wet.shape[2]
    done = share(EARLY_TILES)
    clear(out, slice(0, PAD))
    clear(out, slice(PAD + tall, PAD + tall + PAD))

    @pl.when(done == 0)
    def _():
        clear(south, slice(0, PAD))

    def body(r, carry):
        faces = whole(east), whole(north), whole(mask)
        inner_tile(r, c, mix, out, packed, own, terms, wet, mixing, south, *faces)
        return carry

    lax.fori_loop(done, tall // SUB, body, 0)
    for k in range(levels):
        for h in range(2):
            cols = slice(h * LANES, (h + 1) * LANES)
            kept_rows = (
                terms[1, 2, k, h, 0:1, :],
                terms[1, 2, k, h, tall - 2 : tall - 1, :],
                terms[1, 2, k, h, tall - 1 : tall, :],
                terms[1, 1, k, h, tall - 1 : tall, :],
                wet[k, h, 0:1, :],
                wet[k, h, 1:2, :],
                wet[k, h, tall - 2 : tall - 1, :],
                wet[k, h, tall - 1 : tall, :],
            )
            for j, one in enumerate(kept_rows):
                row_own[j * levels + k : j * levels + k + 1, cols] = one


def side_correction(west, east, faces, mine, own):
    slot = slots()
    a, b, g, up = face_terms(rolled(faces, -2), rolled(faces, -3))
    near = rolled(west, 1)
    flux = a * near + b * mine - g * jnp.where(up, rolled(west, 2), rolled(mine, -1))
    mine_g = rolled(own, -4)
    first = jnp.maximum(mine_g, 0.0) * near
    beyond = jnp.minimum(mine_g, 0.0) * rolled(east, -2)
    last = rolled(beyond, 1) + rolled(own, -6) * rolled(east, -1)
    found = jnp.where(slot == 0, flux + first, -rolled(first, 1))
    found = jnp.where(slot < 0, beyond - jnp.where(slot == -1, last, 0.0), found)
    return jnp.where(slot < 2, own * found, 0.0)


def add_sides(get, correction, tl):
    lane = lane_ids()
    here = rolled(correction, -8 * tl)
    return get(0) + jnp.where(lane < 2, here, 0.0), get(1) + jnp.where(lane >= LANES - 2, here, 0.0)


def across_fold(x, index):
    picked = []
    for h in range(2):
        at = jnp.broadcast_to(index[:, h * LANES : (h + 1) * LANES], (SUB, LANES))
        at = lax.bitwise_and(at, 2 * LANES - 1)
        low = lax.bitwise_and(at, LANES - 1)
        parts = [jnp.take_along_axis(x[j], low, axis=1) for j in range(2)]
        picked.append(jnp.where(at < LANES, parts[0], parts[1]))
    return picked


def row_corrections(state, offset, rows_a, rows_b, faces_a, faces_b, row_own, index, tall, levels, apply):
    even_lat = parity("lat")
    lat = lax.axis_index("lat")
    at_top = lat == lax.axis_size("lat") - 1
    at_bottom = lat == 0
    for t in range(TRACERS):
        part = [slice((depth * TRACERS + t) * levels, (depth * TRACERS + t + 1) * levels) for depth in range(2)]
        north, south = [], []
        for depth in range(2):
            one, other = rows_a[part[depth], :], rows_b[part[depth], :]
            upper = jnp.where(even_lat, one, other)
            lower = jnp.where(even_lat, other, one)
            lower = jnp.where(at_bottom, 0.0, lower)
            upper = [upper[:, h * LANES : (h + 1) * LANES] for h in range(2)]
            folded = across_fold(upper, index)
            north.append([jnp.where(at_top, folded[h], upper[h]) for h in range(2)])
            south.append([lower[:, h * LANES : (h + 1) * LANES] for h in range(2)])
        for h in range(2):
            cols = slice(h * LANES, (h + 1) * LANES)
            base = 2 * TRACERS * levels
            faces = []
            for comp in range(2):
                span = slice(base + comp * levels, base + (comp + 1) * levels)
                one = jnp.where(even_lat, faces_b[span, cols], faces_a[span, cols])
                faces.append(jnp.where(at_bottom, 0.0, one))
            kept = [row_own[j * levels : (j + 1) * levels, cols] for j in range(8)]
            bottom = [
                jnp.concatenate([state[t, k, h, offset + j : offset + j + 1, :] for k in range(levels)], axis=0)
                for j in range(2)
            ]
            a, b, g, up = face_terms(faces[0], faces[1])
            flux = a * south[0][h] + b * bottom[0] - g * jnp.where(up, south[1][h], bottom[1])
            first = jnp.maximum(kept[0], 0.0) * south[0][h]
            row0 = kept[4] * (flux + first)
            row1 = -(kept[5] * first)
            last = kept[3] * north[0][h] - jnp.minimum(kept[2], 0.0) * north[1][h]
            before = -(jnp.minimum(kept[1], 0.0) * north[0][h])
            row2 = -(kept[6] * before)
            row3 = kept[7] * (before - last)
            for k in range(levels):
                for at, add in ((0, row0), (1, row1), (tall - 2, row2), (tall - 1, row3)):
                    apply(t, k, h, at, add[k : k + 1, :])


def received(side_a, side_b, rows, even_lon):
    one, other = side_a[rows, :], side_b[rows, :]
    return jnp.where(even_lon, other, one), jnp.where(even_lon, one, other)


def add_rows(state, offset):
    def apply(t, k, h, at, add):
        spot = (t, k, h, slice(offset + at, offset + at + 1), slice(None))
        state[spot] = state[spot] + add

    return apply


def edge_kernel(
    got_a, got_b, sent, rows_a, rows_b, own, row_own, packed, index, before, c_in,
    c, next_side, next_side_again, next_rows_a, next_rows_b, correction,
):
    levels, tall = before.shape[1], own.shape[0]
    tiles = tall // SUB
    even_lon = parity("lon")

    def one_tile(r):
        rows = tile_rows(r)
        west, east = received(got_a, got_b, rows, even_lon)
        return side_correction(west, east, west, sent[rows, :], own[rows, :])

    def middle(r, carry):
        rows = tile_rows(r)
        found = one_tile(r)
        correction[rows, :] = found
        next_side[rows, :] = packed[rows, :] + found
        next_side_again[rows, :] = packed[rows, :] + found
        return carry

    lax.fori_loop(1, tiles - 1, middle, 0, unroll=True)
    row_corrections(before, PAD, rows_a, rows_b, rows_a, rows_b, row_own, index, tall, levels, add_rows(c, PAD))
    for r in (0, tiles - 1):
        rows = tile_rows(r)
        found = one_tile(r)
        correction[rows, :] = jnp.zeros((SUB, LANES), F32)
        fix_tile(c, r, found, levels)
        sides = packed_edges(lambda t, k, h: c[t, k, h, tile_rows(r, PAD), :], levels)
        next_side[rows, :] = sides
        next_side_again[rows, :] = sides
    send_rows(c, next_rows_a, next_rows_b, levels, tall)


def fix_tile(c, r, found, levels):
    for t in range(TRACERS):
        for k in range(levels):
            new = add_sides(lambda h: c[t, k, h, tile_rows(r, PAD), :], found, t * levels + k)
            for h in range(2):
                c[t, k, h, tile_rows(r, PAD), :] = new[h]


def second_turns(c, correction, terms, wet, mixing, out, south, east_next, east_far, along):
    levels, tall = wet.shape[0], wet.shape[2]
    tiles = tall // SUB
    whole = (c, east_next, east_far, along, south, terms, wet, mixing, out, correction)
    more = (2 * PAD, 0, 0, 0, PAD, 0, 0, 0, 0, 0)

    def turn(i, count, refs):
        c, east_next, east_far, along, south, terms, wet, mixing, out, correction = refs
        step = Step(c, east_next, east_far, along, south, terms, wet, mixing, out, 0)

        def ready(i, ahead, k, t):
            rows = tile_rows(i, PAD + ahead * SUB)
            found = correction[tile_rows(i, ahead * SUB), :]
            new = add_sides(lambda h: c[t, k, h, rows, :], found, t * levels + k)
            for h in range(2):
                c[t, k, h, rows, :] = new[h]

        step.turn(i, count, ready)

    def begin():
        for t in range(TRACERS):
            for k in range(levels):
                for h in range(2):
                    south[t, k, h, 0:PAD, :] = jnp.zeros((PAD, LANES), F32)
        for i in range(-1, FIRST_TURN):
            turn(i, tiles, whole)

    def middle(lo, hi):
        def body(i, carry):
            turn(3, WINDOW, windows(i, whole, more))
            return carry

        lax.fori_loop(lo, hi, body, 0)

    def end():
        for i in range(tiles - 1, tiles + 2):
            turn(i, tiles, whole)

    return begin, middle, end


FIRST_TURN = 3


def second_early_kernel(
    c_in, side_in, side_again_in, rows_a_in, rows_b_in, correction, terms, wet, mixing,
    c, side, side_again, rows_a, rows_b, out, south, east_next, east_far, along,
):
    count = share(EARLY_TURNS)
    begin, middle, _ = second_turns(c, correction, terms, wet, mixing, out, south, east_next, east_far, along)

    @pl.when(count > 0)
    def _():
        begin()
        middle(FIRST_TURN, FIRST_TURN + count)


def second_kernel(
    c_in, out_in, south_in, east_next_in, east_far_in, along_in, correction, terms, wet, mixing,
    c, out, south, east_next, east_far, along,
):
    count = share(EARLY_TURNS)
    begin, middle, end = second_turns(c, correction, terms, wet, mixing, out, south, east_next, east_far, along)

    @pl.when(count == 0)
    def _():
        begin()

    middle(FIRST_TURN + count, wet.shape[2] // SUB - 1)
    end()


def last_kernel(
    got_a, got_b, sent, first_a, first_b, rows_a, rows_b, faces_a, faces_b, own, row_own, index, before, wet, c_in,
    fields, density, c, fields_out, density_out, sems,
):
    levels, tall = before.shape[1], own.shape[0]
    even_lon = parity("lon")
    row_corrections(before, PAD, rows_a, rows_b, faces_a, faces_b, row_own, index, tall, levels, add_rows(c, 0))

    def body(r, carry):
        rows = tile_rows(r)
        west, east = received(got_a, got_b, rows, even_lon)
        faces, _ = received(first_a, first_b, rows, even_lon)
        found = side_correction(west, east, faces, sent[rows, :], own[rows, :])
        for k in range(levels):
            new = [add_sides(lambda h: c[t, k, h, rows, :], found, t * levels + k) for t in range(TRACERS)]
            for h in range(2):
                for t in range(TRACERS):
                    fields_out[t, k, h, rows, :] = new[t][h]
                heat, salt = new[0][h], new[1][h]
                density_out[k, h, rows, :] = wet[k, h, rows, :] * (0.8 * salt - 0.2 * heat - 0.05 * heat * heat)
        return carry

    cuts = [0, 40, 80, 120, tall]
    copies = []
    for i, (lo, hi) in enumerate(zip(cuts[:-1], cuts[1:])):
        lax.fori_loop(lo // SUB, hi // SUB, body, 0, unroll=True)
        for h in range(2):
            cols = slice(h * LANES, (h + 1) * LANES)
            copies.append(
                pltpu.make_async_copy(
                    fields_out.at[:, :, h, lo:hi, :], fields.at[:, :, lo:hi, cols], sems.at[4 * i + h]
                )
            )
            copies.append(
                pltpu.make_async_copy(
                    density_out.at[:, h, lo:hi, :], density.at[:, lo:hi, cols], sems.at[4 * i + 2 + h]
                )
            )
        for one in copies[-4:]:
            one.start()
    for one in copies:
        one.wait()


def vmem(*shape, dtype=F32):
    return pltpu.VMEM(shape, dtype)


ON_CHIP = pl.BlockSpec(memory_space=pltpu.VMEM)
ANYWHERE = pl.BlockSpec(memory_space=pltpu.HBM)
SCALARS = pl.BlockSpec(memory_space=pltpu.SMEM)


def call(kernel, ins, out_shape, out_specs, scratch, cost, aliases=None):
    return pl.pallas_call(
        kernel,
        out_shape=out_shape,
        in_specs=ins,
        out_specs=out_specs,
        scratch_shapes=scratch,
        input_output_aliases=aliases or {},
        cost_estimate=pl.CostEstimate(flops=cost[0], bytes_accessed=cost[1], transcendentals=0),
        compiler_params=pltpu.CompilerParams(vmem_limit_bytes=VMEM_BYTES),
    )


def pairings(lats, lons):
    place = lambda a, o: (a % lats) * lons + o % lons
    by = {"lon_a": [], "lon_b": [], "lat_a": [], "lat_b": []}
    for a in range(lats):
        for o in range(lons):
            me = place(a, o)
            by["lon_a"].append((me, place(a, o ^ 1)))
            by["lon_b"].append((me, place(a, o + 1 if o % 2 else o - 1)))
            by["lat_a"].append((me, place(a ^ 1, o)))
            if a == lats - 1:
                other = place(a, lons - 1 - o)
            elif a == 0:
                other = place(a, o ^ 1)
            else:
                other = place(a + 1 if a % 2 else a - 1, o)
            by["lat_b"].append((me, other))
    return by


def on_device(pairs, tracers, east_faces, north_faces, land_mask, fold_partner, vert_mix):
    _, levels, tall, wide = tracers.shape
    assert wide == 2 * LANES and TRACERS * levels * 8 == LANES and tall % SUB == 0
    index = fold_partner.reshape(1, wide)
    both = ("lat", "lon")
    swap = lambda x, name: lax.ppermute(x, both, pairs[name])
    near = [pltpu.with_memory_space_constraint(x, pltpu.VMEM) for x in (east_faces, north_faces, land_mask)]
    tracers, east_faces, north_faces, land_mask = (
        pltpu.with_memory_space_constraint(x, pltpu.HBM) for x in (tracers, east_faces, north_faces, land_mask)
    )
    state = vmem(TRACERS, levels, 2, tall + 2 * PAD, LANES)
    side, rows3, rows2 = vmem(tall, LANES), vmem(6 * levels, wide), vmem(4 * levels, wide)
    faces = vmem(2, levels, 2, tall, LANES)
    level = vmem(levels, 2, tall, LANES)
    grid = vmem(TRACERS, levels, 2, tall, LANES)
    grid_bytes = tracers.size * 4

    c0, sent, sent_again, rows_a, rows_b = call(
        start_kernel,
        [ANYWHERE] * 3,
        [state, side, side, rows3, rows3],
        [ON_CHIP] * 5,
        [vmem(2, levels, tall, LANES), vmem(2, levels, SUB, wide), pltpu.SemaphoreType.DMA((13,))],
        (1000000, 2 * grid_bytes),
    )(tracers, east_faces, north_faces)
    got_a, got_rows_a = swap(sent, "lon_a"), swap(rows_a, "lat_a")
    assert REST_PIECES[-1][1] == tall
    shared = [state, side, side, vmem(2, 3, levels, 2, tall, LANES), level, vmem(levels - 1, 2, tall, LANES),
              vmem(TRACERS, levels, 2, tall + PAD, LANES)]
    early_rows = FIRST_PIECES[-1][1]
    *state_so_far, sent_again, rows_b = call(
        early_kernel,
        [ON_CHIP, ANYWHERE, ANYWHERE, ANYWHERE, SCALARS, ON_CHIP, ON_CHIP],
        shared + [side, rows3],
        [ON_CHIP] * 9,
        [vmem(2, levels, 2, early_rows, LANES)] * 2
        + [vmem(levels, 2, early_rows, LANES, dtype=jnp.int32), pltpu.SemaphoreType.DMA((12,))],
        (10000000, grid_bytes),
        {5: 7, 6: 8},
    )(c0, east_faces, north_faces, land_mask, vert_mix, sent_again, rows_b)
    got_b, got_rows_b = swap(sent_again, "lon_b"), swap(rows_b, "lat_b")
    c1, packed, own, terms, wet, mixing, _, row_own = call(
        inner_kernel,
        [ON_CHIP] * 4 + [SCALARS] + [ON_CHIP] * 7,
        shared + [vmem(8 * levels, wide)],
        [ON_CHIP] * 8,
        [],
        (40000000, 4 * grid_bytes),
        {5 + j: j for j in range(7)},
    )(c0, *near, vert_mix, *state_so_far)
    c1, next_side, next_again, next_rows_a, next_rows_b, correction = call(
        edge_kernel,
        [ON_CHIP] * 11,
        [state, side, side, rows2, rows2, side],
        [ON_CHIP] * 6,
        [],
        (1000000, 1000000),
        {10: 0},
    )(got_a, got_b, sent, got_rows_a, got_rows_b, own, row_own, packed, index, c0, c1)
    kept = [grid, vmem(TRACERS, levels, 2, tall + PAD, LANES), grid, grid, grid]
    c1, sent_side, sent_side_again, next_rows_a, next_rows_b, *kept_so_far = call(
        second_early_kernel,
        [ON_CHIP] * 9,
        [state, side, side, rows2, rows2] + kept,
        [ON_CHIP] * 10,
        [],
        (10000000, grid_bytes),
        {j: j for j in range(5)},
    )(c1, next_side, next_again, next_rows_a, next_rows_b, correction, terms, wet, mixing)
    new_a, new_b = swap(sent_side, "lon_a"), swap(sent_side_again, "lon_b")
    new_rows_a, new_rows_b = swap(next_rows_a, "lat_a"), swap(next_rows_b, "lat_b")
    c1, c2, *_ = call(
        second_kernel,
        [ON_CHIP] * 10,
        [state] + kept,
        [ON_CHIP] * 6,
        [],
        (40000000, 4 * grid_bytes),
        {j: j for j in range(6)},
    )(c1, *kept_so_far, correction, terms, wet, mixing)
    fields, density, _ = call(
        last_kernel,
        [ON_CHIP] * 15,
        [
            jax.ShapeDtypeStruct(tracers.shape, F32),
            jax.ShapeDtypeStruct(land_mask.shape, F32),
            vmem(TRACERS, levels, 2, tall, LANES),
        ],
        [ANYWHERE, ANYWHERE, ON_CHIP],
        [vmem(TRACERS, levels, 2, tall, LANES), level, pltpu.SemaphoreType.DMA((16,))],
        (4000000, 2 * grid_bytes),
        {14: 2},
    )(
        new_a, new_b, sent_side, got_a, got_b, new_rows_a, new_rows_b, got_rows_a, got_rows_b,
        own, row_own, index, c1, wet, c2,
    )
    return fields, density


def solution(mesh):
    in_specs = (
        P(None, None, "lat", "lon"),
        P(None, None, "lat", "lon"),
        P(None, None, "lat", "lon"),
        P(None, "lat", "lon"),
        P("lon"),
        P(),
    )
    out_specs = (P(None, None, "lat", "lon"), P(None, "lat", "lon"))
    pairs = pairings(mesh.shape["lat"], mesh.shape["lon"])

    def body(*args):
        return on_device(pairs, *args)

    return jax.shard_map(body, mesh=mesh, in_specs=in_specs, out_specs=out_specs, check_vma=False)
```

```python
import jax
import jax.numpy as jnp
from jax import lax
from jax.experimental import pallas as pl
from jax.experimental.pallas import tpu as pltpu
from jax.sharding import PartitionSpec as P

F32 = jnp.float32
LANES = 128
SUB = 8
PAD = 8
TRACERS = 2
VMEM_BYTES = 14 * 1024 * 1024


def lane_ids():
    return lax.broadcasted_iota(jnp.int32, (SUB, LANES), 1)


def rolled(x, by):
    by = by % LANES
    return x if by == 0 else pltpu.roll(x, by, 1)


def face_terms(flow, spread):
    g = 0.125 * flow
    up = flow > 0.0
    g3 = 3.0 * g
    g6 = 6.0 * g
    return jnp.where(up, g6, g3) + spread, jnp.where(up, g3, g6) - spread, g, up


def tile_rows(index, offset=0):
    if isinstance(index, int):
        return pl.ds(index * SUB + offset, SUB)
    return pl.ds(pl.multiple_of(index * SUB, SUB) + offset, SUB)


def set_terms(r, east, north, mask, mix, terms, wet, mixing):
    levels = wet.shape[0]
    rows = tile_rows(r)
    for h in range(2):
        cells = [mask(k, h, rows).astype(F32) for k in range(levels)]
        for k in range(levels):
            wet[k, h, rows, :] = cells[k]
            if k + 1 < levels:
                mixing[k, h, rows, :] = mix[k] * cells[k] * cells[k + 1]
            for way, faces in enumerate((east, north)):
                a, b, g, _ = face_terms(faces(0, k, h, rows), faces(1, k, h, rows))
                for j, one in enumerate((a, b, g)):
                    terms[way, j, k, h, rows, :] = one


def halved(ref):
    return lambda *at: ref[at + (slice(None),)]


def whole(ref):
    return lambda *at: ref[at[:-2] + (at[-1], slice(at[-2] * LANES, (at[-2] + 1) * LANES))]


def advance_tile(r, c, south, terms, wet, mixing, out, out_pad):
    levels = wet.shape[0]
    lane = lane_ids()
    first, last, last2 = lane > 0, lane < LANES - 1, lane < LANES - 2
    rows = tile_rows(r)

    def cells(t, k, h, by=0):
        return c[t, k, h, tile_rows(r, PAD + by), :]

    for k in range(levels):
        for h in range(2):
            a, b, g = (terms[1, j, k, h, rows, :] for j in range(3))
            up = g > 0.0
            for t in range(TRACERS):
                further = jnp.where(up, cells(t, k, h, -1), cells(t, k, h, 2))
                face = a * cells(t, k, h) + b * cells(t, k, h, 1) - g * further
                south[t, k, h, tile_rows(r, PAD), :] = face
    below = [[None] * 2 for _ in range(TRACERS)]
    for k in range(levels):
        for t in range(TRACERS):
            c0 = [cells(t, k, h) for h in range(2)]
            plus1 = [rolled(x, -1) for x in c0]
            plus2 = [rolled(x, -2) for x in c0]
            minus1 = [rolled(x, 1) for x in c0]
            p1 = jnp.where(last, plus1[0], plus1[1]), jnp.where(last, plus1[1], 0.0)
            p2 = jnp.where(last2, plus2[0], plus2[1]), jnp.where(last2, plus2[1], 0.0)
            m1 = jnp.where(first, minus1[0], 0.0), jnp.where(first, minus1[1], minus1[0])
            flux = []
            for h in range(2):
                a, b, g = (terms[0, j, k, h, rows, :] for j in range(3))
                flux.append(a * c0[h] + b * p1[h] - g * jnp.where(g > 0.0, m1[h], p2[h]))
            shifted = [rolled(x, 1) for x in flux]
            west = jnp.where(first, shifted[0], 0.0), jnp.where(first, shifted[1], shifted[0])
            for h in range(2):
                change = west[h] - flux[h]
                change = change + (south[t, k, h, tile_rows(r, PAD - 1), :] - south[t, k, h, tile_rows(r, PAD), :])
                if k + 1 < levels:
                    vertical = mixing[k, h, rows, :] * (cells(t, k + 1, h) - c0[h])
                    change = change + vertical
                if k > 0:
                    change = change - below[t][h]
                if k + 1 < levels:
                    below[t][h] = vertical
                out[t, k, h, tile_rows(r, out_pad), :] = c0[h] + wet[k, h, rows, :] * change


class Step:
    def __init__(self, c, east_next, east_far, along, south, terms, wet, mixing, out, out_pad):
        self.c, self.east_next, self.east_far, self.along, self.south = c, east_next, east_far, along, south
        self.terms, self.wet, self.mixing, self.out, self.out_pad = terms, wet, mixing, out, out_pad
        self.levels = wet.shape[0]
        self.below = {}

    def cells(self, t, k, h, i, ahead, by=0):
        return self.c[t, k, h, tile_rows(i, PAD + ahead * SUB + by), :]

    def neighbours(self, i, ahead, k, t):
        lane = lane_ids()
        first, last, last2 = lane > 0, lane < LANES - 1, lane < LANES - 2
        rows = tile_rows(i, ahead * SUB)
        c0 = [self.cells(t, k, h, i, ahead) for h in range(2)]
        plus1 = [rolled(x, -1) for x in c0]
        plus2 = [rolled(x, -2) for x in c0]
        minus1 = [rolled(x, 1) for x in c0]
        p1 = jnp.where(last, plus1[0], plus1[1]), jnp.where(last, plus1[1], 0.0)
        p2 = jnp.where(last2, plus2[0], plus2[1]), jnp.where(last2, plus2[1], 0.0)
        m1 = jnp.where(first, minus1[0], 0.0), jnp.where(first, minus1[1], minus1[0])
        for h in range(2):
            self.east_next[t, k, h, rows, :] = p1[h]
            self.east_far[t, k, h, rows, :] = jnp.where(self.terms[0, 2, k, h, rows, :] > 0.0, m1[h], p2[h])

    def fluxes(self, i, ahead, k, t):
        first = lane_ids() > 0
        rows = tile_rows(i, ahead * SUB)
        flux = []
        for h in range(2):
            a, b, g = (self.terms[0, j, k, h, rows, :] for j in range(3))
            flux.append(
                a * self.cells(t, k, h, i, ahead)
                + b * self.east_next[t, k, h, rows, :]
                - g * self.east_far[t, k, h, rows, :]
            )
        shifted = [rolled(x, 1) for x in flux]
        west = jnp.where(first, shifted[0], 0.0), jnp.where(first, shifted[1], shifted[0])
        for h in range(2):
            self.along[t, k, h, rows, :] = west[h] - flux[h]
            a, b, g = (self.terms[1, j, k, h, rows, :] for j in range(3))
            further = jnp.where(g > 0.0, self.cells(t, k, h, i, ahead, -1), self.cells(t, k, h, i, ahead, 2))
            self.south[t, k, h, tile_rows(i, PAD + ahead * SUB), :] = (
                a * self.cells(t, k, h, i, ahead) + b * self.cells(t, k, h, i, ahead, 1) - g * further
            )

    def finish(self, i, ahead, k, t):
        rows = tile_rows(i, ahead * SUB)
        for h in range(2):
            c0 = self.cells(t, k, h, i, ahead)
            change = self.along[t, k, h, rows, :] + (
                self.south[t, k, h, tile_rows(i, PAD + ahead * SUB - 1), :]
                - self.south[t, k, h, tile_rows(i, PAD + ahead * SUB), :]
            )
            if k > 0:
                change = change - self.below[t, h]
            if k + 1 < self.levels:
                self.below[t, h] = self.mixing[k, h, rows, :] * (self.cells(t, k + 1, h, i, ahead) - c0)
                change = change + self.below[t, h]
            place = tile_rows(i, self.out_pad + ahead * SUB)
            self.out[t, k, h, place, :] = c0 + self.wet[k, h, rows, :] * change

    def turn(self, i, tiles, before=None, after=None):
        inside = lambda ahead: 0 <= i + ahead < tiles
        packs = after(i, -3) if after is not None and inside(-3) else None
        for k in range(self.levels):
            for t in range(TRACERS):
                if inside(-2):
                    self.finish(i, -2, k, t)
                if inside(-1):
                    self.fluxes(i, -1, k, t)
                if inside(0):
                    self.neighbours(i, 0, k, t)
                if before is not None and inside(1):
                    before(i, 1, k, t)
            if packs is not None:
                packs(k)


WINDOW = 5


def windows(i, refs, more):
    start = pl.multiple_of((i - 3) * SUB, SUB)
    seen = []
    for ref, rows in zip(refs, more):
        before = (slice(None),) * (len(ref.shape) - 2)
        seen.append(ref.at[before + (pl.ds(start, WINDOW * SUB + rows), slice(None))])
    return seen


def group(tl):
    lane = lane_ids()
    return lax.bitwise_and(lax.shift_right_logical(lane + 2, 3), LANES // SUB - 1) == tl


def slots():
    return lax.bitwise_and(lane_ids() + 2, 7) - 2


def packed_edges(get, levels, extra=None):
    lane = lane_ids()
    packed = jnp.zeros((SUB, LANES), F32)
    for t in range(TRACERS):
        for k in range(levels):
            tl = t * levels + k
            one = jnp.where(lane >= LANES - 2, get(t, k, 1), get(t, k, 0))
            if extra is not None:
                one = jnp.where(jnp.logical_and(lane >= 2, lane < 4), extra[k], one)
            packed = jnp.where(group(tl), rolled(one, 8 * tl), packed)
    return packed


def parity(axis):
    return lax.rem(lax.axis_index(axis), 2) == 0


def start_kernel(tracers, east, north, c, side, side_again, rows_a, rows_b, east_last, north_top, sems):
    levels, tall = tracers.shape[1], tracers.shape[2]
    cuts = [0, 48, 96, tall]
    copies = []
    for i, (lo, hi) in enumerate(zip(cuts[:-1], cuts[1:])):
        group_of = []
        for h in range(2):
            group_of.append(
                pltpu.make_async_copy(
                    tracers.at[:, :, lo:hi, h * LANES : (h + 1) * LANES],
                    c.at[:, :, h, PAD + lo : PAD + hi, :],
                    sems.at[3 * i + h],
                )
            )
        group_of.append(
            pltpu.make_async_copy(
                east.at[:, :, lo:hi, LANES:], east_last.at[:, :, lo:hi, :], sems.at[3 * i + 2]
            )
        )
        copies.append(group_of)
    top_copy = pltpu.make_async_copy(north.at[:, :, tall - SUB :, :], north_top, sems.at[9])
    for group_of in copies:
        for one in group_of:
            one.start()
    top_copy.start()
    for t in range(TRACERS):
        for k in range(levels):
            for h in range(2):
                c[t, k, h, 0:PAD, :] = jnp.zeros((PAD, LANES), F32)
                c[t, k, h, PAD + tall :, :] = jnp.zeros((PAD, LANES), F32)
    lane = lane_ids()

    def pack(r, carry):
        rows = tile_rows(r)
        faces = []
        for k in range(levels):
            faces.append(
                jnp.where(lane == 2, rolled(east_last[0, k, rows, :], 3), rolled(east_last[1, k, rows, :], 4))
            )
        side[rows, :] = packed_edges(lambda t, k, h: c[t, k, h, tile_rows(r, PAD), :], levels, faces)
        side_again[rows, :] = side[rows, :]
        return carry

    for i, (lo, hi) in enumerate(zip(cuts[:-1], cuts[1:])):
        for one in copies[i]:
            one.wait()
        lax.fori_loop(lo // SUB, hi // SUB, pack, 0, unroll=True)
    top_copy.wait()
    send_rows(c, rows_a, rows_b, levels, tall)
    for comp in range(2):
        for k in range(levels):
            one_row = north_top[comp, k, SUB - 1 : SUB, :]
            at = 2 * TRACERS * levels + comp * levels + k
            rows_a[at : at + 1, :] = one_row
            rows_b[at : at + 1, :] = one_row


def send_rows(c, rows_a, rows_b, levels, tall):
    even_lat = parity("lat")
    for depth in range(2):
        top, bottom = PAD + tall - 1 - depth, PAD + depth
        at_a = jnp.where(even_lat, top, bottom)
        at_b = jnp.where(even_lat, bottom, top)
        for t in range(TRACERS):
            for k in range(levels):
                tl = (depth * TRACERS + t) * levels + k
                for h in range(2):
                    cols = slice(h * LANES, (h + 1) * LANES)
                    rows_a[tl : tl + 1, cols] = c[t, k, h, pl.ds(at_a, 1), :]
                    rows_b[tl : tl + 1, cols] = c[t, k, h, pl.ds(at_b, 1), :]


def inner_copies(pieces, east, north, mask, east_in, north_in, mask_in, sems):
    copies = []
    for i, (lo, hi) in enumerate(pieces):
        group_of = []
        for h in range(2):
            cols = slice(h * LANES, (h + 1) * LANES)
            for j, (src, dst) in enumerate(((east, east_in), (north, north_in))):
                group_of.append(
                    pltpu.make_async_copy(
                        src.at[:, :, lo:hi, cols], dst.at[:, :, h, lo:hi, :], sems.at[6 * i + 3 * h + j]
                    )
                )
            group_of.append(
                pltpu.make_async_copy(
                    mask.at[:, lo:hi, cols], mask_in.at[:, h, lo:hi, :], sems.at[6 * i + 3 * h + 2]
                )
            )
        copies.append(group_of)
    return copies


def clear(ref, rows):
    for t in range(TRACERS):
        for k in range(ref.shape[1]):
            for h in range(2):
                ref[t, k, h, rows, :] = jnp.zeros((PAD, LANES), F32)


def inner_tile(r, c, mix, out, packed, own, terms, wet, mixing, south, east_in, north_in, mask_in):
    levels = wet.shape[0]
    lane = lane_ids()
    rows = tile_rows(r)
    set_terms(r, east_in, north_in, mask_in, mix, terms, wet, mixing)
    advance_tile(r, c, south, terms, wet, mixing, out, PAD)
    packed[rows, :] = packed_edges(lambda t, k, h: out[t, k, h, tile_rows(r, PAD), :], levels)
    kept = jnp.zeros((SUB, LANES), F32)
    edge = lane >= LANES - 2
    for k in range(levels):
        one = jnp.where(edge, wet[k, 1, rows, :], wet[k, 0, rows, :])
        g = jnp.where(edge, terms[0, 2, k, 1, rows, :], terms[0, 2, k, 0, rows, :])
        some = jnp.where(lane == 5, rolled(terms[0, 1, k, 1, rows, :], 6), rolled(g, 4))
        one = jnp.where(jnp.logical_and(lane >= 2, lane < 6), some, one)
        kept = jnp.where(group(k), rolled(one, 8 * k), kept)
    own[rows, :] = jnp.where(jnp.logical_or(lane < LANES // 2 - 2, edge), kept, rolled(kept, LANES // 2))


FIRST_PIECES = ((0, 24), (24, 64))
REST_PIECES = ((64, 88), (88, 120), (120, 152))


def share(parts):
    place = lax.axis_index("lon") // 2
    amount = jnp.int32(0)
    for i, part in enumerate(parts):
        amount = jnp.where(place == i, part, amount)
    return amount


EARLY_TILES = (8, 5, 3, 2)
EARLY_TURNS = (10, 6, 3, 1)


def early_kernel(
    c, east, north, mask, mix, side_in, rows_in,
    out, packed, own, terms, wet, mixing, south, side, rows_b, east_in, north_in, mask_in, sems,
):
    count = share(EARLY_TILES)

    @pl.when(count > 0)
    def _():
        clear(south, slice(0, PAD))
        run_pieces(
            FIRST_PIECES, c, east, north, mask, mix, out, packed, own, terms, wet, mixing, south,
            east_in, north_in, mask_in, sems, count,
        )


def run_pieces(
    pieces, c, east, north, mask, mix, out, packed, own, terms, wet, mixing, south, east_in, north_in, mask_in, sems,
    count,
):
    copies = inner_copies(pieces, east, north, mask, east_in, north_in, mask_in, sems)

    def body(r, carry):
        faces = halved(east_in), halved(north_in), halved(mask_in)
        inner_tile(r, c, mix, out, packed, own, terms, wet, mixing, south, *faces)
        return carry

    for group_of in copies:
        for one in group_of:
            one.start()
    for (lo, hi), group_of in zip(pieces, copies):
        for one in group_of:
            one.wait()
        lax.fori_loop(lo // SUB, jnp.minimum(hi // SUB, count), body, 0)


def inner_kernel(
    c, east, north, mask, mix, out_in, packed_in, own_in, terms_in, wet_in, mixing_in, south_in,
    out, packed, own, terms, wet, mixing, south, row_own,
):
    levels, tall = wet.shape[0], wet.shape[2]
    done = share(EARLY_TILES)
    clear(out, slice(0, PAD))
    clear(out, slice(PAD + tall, PAD + tall + PAD))

    @pl.when(done == 0)
    def _():
        clear(south, slice(0, PAD))

    def body(r, carry):
        faces = whole(east), whole(north), whole(mask)
        inner_tile(r, c, mix, out, packed, own, terms, wet, mixing, south, *faces)
        return carry

    lax.fori_loop(done, tall // SUB, body, 0)
    for k in range(levels):
        for h in range(2):
            cols = slice(h * LANES, (h + 1) * LANES)
            kept_rows = (
                terms[1, 2, k, h, 0:1, :],
                terms[1, 2, k, h, tall - 2 : tall - 1, :],
                terms[1, 2, k, h, tall - 1 : tall, :],
                terms[1, 1, k, h, tall - 1 : tall, :],
                wet[k, h, 0:1, :],
                wet[k, h, 1:2, :],
                wet[k, h, tall - 2 : tall - 1, :],
                wet[k, h, tall - 1 : tall, :],
            )
            for j, one in enumerate(kept_rows):
                row_own[j * levels + k : j * levels + k + 1, cols] = one


def side_correction(west, east, faces, mine, own):
    slot = slots()
    a, b, g, up = face_terms(rolled(faces, -2), rolled(faces, -3))
    near = rolled(west, 1)
    flux = a * near + b * mine - g * jnp.where(up, rolled(west, 2), rolled(mine, -1))
    mine_g = rolled(own, -4)
    first = jnp.maximum(mine_g, 0.0) * near
    beyond = jnp.minimum(mine_g, 0.0) * rolled(east, -2)
    last = rolled(beyond, 1) + rolled(own, -6) * rolled(east, -1)
    found = jnp.where(slot == 0, flux + first, -rolled(first, 1))
    found = jnp.where(slot < 0, beyond - jnp.where(slot == -1, last, 0.0), found)
    return jnp.where(slot < 2, own * found, 0.0)


def add_sides(get, correction, tl):
    lane = lane_ids()
    here = rolled(correction, -8 * tl)
    return get(0) + jnp.where(lane < 2, here, 0.0), get(1) + jnp.where(lane >= LANES - 2, here, 0.0)


def across_fold(x, index):
    picked = []
    for h in range(2):
        at = jnp.broadcast_to(index[:, h * LANES : (h + 1) * LANES], (SUB, LANES))
        at = lax.bitwise_and(at, 2 * LANES - 1)
        low = lax.bitwise_and(at, LANES - 1)
        parts = [jnp.take_along_axis(x[j], low, axis=1) for j in range(2)]
        picked.append(jnp.where(at < LANES, parts[0], parts[1]))
    return picked


def row_corrections(state, offset, rows_a, rows_b, faces_a, faces_b, row_own, index, tall, levels, apply):
    even_lat = parity("lat")
    lat = lax.axis_index("lat")
    at_top = lat == lax.axis_size("lat") - 1
    at_bottom = lat == 0
    for t in range(TRACERS):
        part = [slice((depth * TRACERS + t) * levels, (depth * TRACERS + t + 1) * levels) for depth in range(2)]
        north, south = [], []
        for depth in range(2):
            one, other = rows_a[part[depth], :], rows_b[part[depth], :]
            upper = jnp.where(even_lat, one, other)
            lower = jnp.where(even_lat, other, one)
            lower = jnp.where(at_bottom, 0.0, lower)
            upper = [upper[:, h * LANES : (h + 1) * LANES] for h in range(2)]
            folded = across_fold(upper, index)
            north.append([jnp.where(at_top, folded[h], upper[h]) for h in range(2)])
            south.append([lower[:, h * LANES : (h + 1) * LANES] for h in range(2)])
        for h in range(2):
            cols = slice(h * LANES, (h + 1) * LANES)
            base = 2 * TRACERS * levels
            faces = []
            for comp in range(2):
                span = slice(base + comp * levels, base + (comp + 1) * levels)
                one = jnp.where(even_lat, faces_b[span, cols], faces_a[span, cols])
                faces.append(jnp.where(at_bottom, 0.0, one))
            kept = [row_own[j * levels : (j + 1) * levels, cols] for j in range(8)]
            bottom = [
                jnp.concatenate([state[t, k, h, offset + j : offset + j + 1, :] for k in range(levels)], axis=0)
                for j in range(2)
            ]
            a, b, g, up = face_terms(faces[0], faces[1])
            flux = a * south[0][h] + b * bottom[0] - g * jnp.where(up, south[1][h], bottom[1])
            first = jnp.maximum(kept[0], 0.0) * south[0][h]
            row0 = kept[4] * (flux + first)
            row1 = -(kept[5] * first)
            last = kept[3] * north[0][h] - jnp.minimum(kept[2], 0.0) * north[1][h]
            before = -(jnp.minimum(kept[1], 0.0) * north[0][h])
            row2 = -(kept[6] * before)
            row3 = kept[7] * (before - last)
            for k in range(levels):
                for at, add in ((0, row0), (1, row1), (tall - 2, row2), (tall - 1, row3)):
                    apply(t, k, h, at, add[k : k + 1, :])


def received(side_a, side_b, rows, even_lon):
    one, other = side_a[rows, :], side_b[rows, :]
    return jnp.where(even_lon, other, one), jnp.where(even_lon, one, other)


def add_rows(state, offset):
    def apply(t, k, h, at, add):
        spot = (t, k, h, slice(offset + at, offset + at + 1), slice(None))
        state[spot] = state[spot] + add

    return apply


def edge_kernel(
    got_a, got_b, sent, rows_a, rows_b, own, row_own, packed, index, before, c_in,
    c, next_side, next_side_again, next_rows_a, next_rows_b, correction,
):
    levels, tall = before.shape[1], own.shape[0]
    tiles = tall // SUB
    even_lon = parity("lon")

    def one_tile(r):
        rows = tile_rows(r)
        west, east = received(got_a, got_b, rows, even_lon)
        return side_correction(west, east, west, sent[rows, :], own[rows, :])

    def middle(r, carry):
        rows = tile_rows(r)
        found = one_tile(r)
        correction[rows, :] = found
        next_side[rows, :] = packed[rows, :] + found
        next_side_again[rows, :] = packed[rows, :] + found
        return carry

    lax.fori_loop(1, tiles - 1, middle, 0, unroll=True)
    row_corrections(before, PAD, rows_a, rows_b, rows_a, rows_b, row_own, index, tall, levels, add_rows(c, PAD))
    for r in (0, tiles - 1):
        rows = tile_rows(r)
        found = one_tile(r)
        correction[rows, :] = jnp.zeros((SUB, LANES), F32)
        fix_tile(c, r, found, levels)
        sides = packed_edges(lambda t, k, h: c[t, k, h, tile_rows(r, PAD), :], levels)
        next_side[rows, :] = sides
        next_side_again[rows, :] = sides
    send_rows(c, next_rows_a, next_rows_b, levels, tall)


def fix_tile(c, r, found, levels):
    for t in range(TRACERS):
        for k in range(levels):
            new = add_sides(lambda h: c[t, k, h, tile_rows(r, PAD), :], found, t * levels + k)
            for h in range(2):
                c[t, k, h, tile_rows(r, PAD), :] = new[h]


def second_turns(c, correction, terms, wet, mixing, out, south, east_next, east_far, along):
    levels, tall = wet.shape[0], wet.shape[2]
    tiles = tall // SUB
    whole = (c, east_next, east_far, along, south, terms, wet, mixing, out, correction)
    more = (2 * PAD, 0, 0, 0, PAD, 0, 0, 0, 0, 0)

    def turn(i, count, refs):
        c, east_next, east_far, along, south, terms, wet, mixing, out, correction = refs
        step = Step(c, east_next, east_far, along, south, terms, wet, mixing, out, 0)

        def ready(i, ahead, k, t):
            rows = tile_rows(i, PAD + ahead * SUB)
            found = correction[tile_rows(i, ahead * SUB), :]
            new = add_sides(lambda h: c[t, k, h, rows, :], found, t * levels + k)
            for h in range(2):
                c[t, k, h, rows, :] = new[h]

        step.turn(i, count, ready)

    def begin():
        for t in range(TRACERS):
            for k in range(levels):
                for h in range(2):
                    south[t, k, h, 0:PAD, :] = jnp.zeros((PAD, LANES), F32)
        for i in range(-1, FIRST_TURN):
            turn(i, tiles, whole)

    def middle(lo, hi):
        def body(i, carry):
            turn(3, WINDOW, windows(i, whole, more))
            return carry

        lax.fori_loop(lo, hi, body, 0)

    def end():
        for i in range(tiles - 1, tiles + 2):
            turn(i, tiles, whole)

    return begin, middle, end


FIRST_TURN = 3


def second_early_kernel(
    c_in, side_in, side_again_in, rows_a_in, rows_b_in, correction, terms, wet, mixing,
    c, side, side_again, rows_a, rows_b, out, south, east_next, east_far, along,
):
    count = share(EARLY_TURNS)
    begin, middle, _ = second_turns(c, correction, terms, wet, mixing, out, south, east_next, east_far, along)

    @pl.when(count > 0)
    def _():
        begin()
        middle(FIRST_TURN, FIRST_TURN + count)


def second_kernel(
    c_in, out_in, south_in, east_next_in, east_far_in, along_in, correction, terms, wet, mixing,
    c, out, south, east_next, east_far, along,
):
    count = share(EARLY_TURNS)
    begin, middle, end = second_turns(c, correction, terms, wet, mixing, out, south, east_next, east_far, along)

    @pl.when(count == 0)
    def _():
        begin()

    middle(FIRST_TURN + count, wet.shape[2] // SUB - 1)
    end()


def last_kernel(
    got_a, got_b, sent, first_a, first_b, rows_a, rows_b, faces_a, faces_b, own, row_own, index, before, wet, c_in,
    fields, density, c, fields_out, density_out, sems,
):
    levels, tall = before.shape[1], own.shape[0]
    even_lon = parity("lon")
    row_corrections(before, PAD, rows_a, rows_b, faces_a, faces_b, row_own, index, tall, levels, add_rows(c, 0))

    def body(r, carry):
        rows = tile_rows(r)
        west, east = received(got_a, got_b, rows, even_lon)
        faces, _ = received(first_a, first_b, rows, even_lon)
        found = side_correction(west, east, faces, sent[rows, :], own[rows, :])
        for k in range(levels):
            new = [add_sides(lambda h: c[t, k, h, rows, :], found, t * levels + k) for t in range(TRACERS)]
            for h in range(2):
                for t in range(TRACERS):
                    fields_out[t, k, h, rows, :] = new[t][h]
                heat, salt = new[0][h], new[1][h]
                density_out[k, h, rows, :] = wet[k, h, rows, :] * (0.8 * salt - 0.2 * heat - 0.05 * heat * heat)
        return carry

    cuts = [0, 40, 96, tall]
    copies = []
    for i, (lo, hi) in enumerate(zip(cuts[:-1], cuts[1:])):
        lax.fori_loop(lo // SUB, hi // SUB, body, 0, unroll=True)
        for h in range(2):
            cols = slice(h * LANES, (h + 1) * LANES)
            copies.append(
                pltpu.make_async_copy(
                    fields_out.at[:, :, h, lo:hi, :], fields.at[:, :, lo:hi, cols], sems.at[4 * i + h]
                )
            )
            copies.append(
                pltpu.make_async_copy(
                    density_out.at[:, h, lo:hi, :], density.at[:, lo:hi, cols], sems.at[4 * i + 2 + h]
                )
            )
        for one in copies[-4:]:
            one.start()
    for one in copies:
        one.wait()


def vmem(*shape, dtype=F32):
    return pltpu.VMEM(shape, dtype)


ON_CHIP = pl.BlockSpec(memory_space=pltpu.VMEM)
ANYWHERE = pl.BlockSpec(memory_space=pltpu.HBM)
SCALARS = pl.BlockSpec(memory_space=pltpu.SMEM)


def call(kernel, ins, out_shape, out_specs, scratch, cost, aliases=None):
    return pl.pallas_call(
        kernel,
        out_shape=out_shape,
        in_specs=ins,
        out_specs=out_specs,
        scratch_shapes=scratch,
        input_output_aliases=aliases or {},
        cost_estimate=pl.CostEstimate(flops=cost[0], bytes_accessed=cost[1], transcendentals=0),
        compiler_params=pltpu.CompilerParams(vmem_limit_bytes=VMEM_BYTES),
    )


def pairings(lats, lons):
    place = lambda a, o: (a % lats) * lons + o % lons
    by = {"lon_a": [], "lon_b": [], "lat_a": [], "lat_b": []}
    for a in range(lats):
        for o in range(lons):
            me = place(a, o)
            by["lon_a"].append((me, place(a, o ^ 1)))
            by["lon_b"].append((me, place(a, o + 1 if o % 2 else o - 1)))
            by["lat_a"].append((me, place(a ^ 1, o)))
            if a == lats - 1:
                other = place(a, lons - 1 - o)
            elif a == 0:
                other = place(a, o ^ 1)
            else:
                other = place(a + 1 if a % 2 else a - 1, o)
            by["lat_b"].append((me, other))
    return by


def on_device(pairs, tracers, east_faces, north_faces, land_mask, fold_partner, vert_mix):
    _, levels, tall, wide = tracers.shape
    assert wide == 2 * LANES and TRACERS * levels * 8 == LANES and tall % SUB == 0
    index = fold_partner.reshape(1, wide)
    both = ("lat", "lon")
    swap = lambda x, name: lax.ppermute(x, both, pairs[name])
    near = [pltpu.with_memory_space_constraint(x, pltpu.VMEM) for x in (east_faces, north_faces, land_mask)]
    tracers, east_faces, north_faces, land_mask = (
        pltpu.with_memory_space_constraint(x, pltpu.HBM) for x in (tracers, east_faces, north_faces, land_mask)
    )
    state = vmem(TRACERS, levels, 2, tall + 2 * PAD, LANES)
    side, rows3, rows2 = vmem(tall, LANES), vmem(6 * levels, wide), vmem(4 * levels, wide)
    faces = vmem(2, levels, 2, tall, LANES)
    level = vmem(levels, 2, tall, LANES)
    grid = vmem(TRACERS, levels, 2, tall, LANES)
    grid_bytes = tracers.size * 4

    c0, sent, sent_again, rows_a, rows_b = call(
        start_kernel,
        [ANYWHERE] * 3,
        [state, side, side, rows3, rows3],
        [ON_CHIP] * 5,
        [vmem(2, levels, tall, LANES), vmem(2, levels, SUB, wide), pltpu.SemaphoreType.DMA((10,))],
        (1000000, 2 * grid_bytes),
    )(tracers, east_faces, north_faces)
    got_a, got_rows_a = swap(sent, "lon_a"), swap(rows_a, "lat_a")
    assert REST_PIECES[-1][1] == tall
    shared = [state, side, side, vmem(2, 3, levels, 2, tall, LANES), level, vmem(levels - 1, 2, tall, LANES),
              vmem(TRACERS, levels, 2, tall + PAD, LANES)]
    early_rows = FIRST_PIECES[-1][1]
    *state_so_far, sent_again, rows_b = call(
        early_kernel,
        [ON_CHIP, ANYWHERE, ANYWHERE, ANYWHERE, SCALARS, ON_CHIP, ON_CHIP],
        shared + [side, rows3],
        [ON_CHIP] * 9,
        [vmem(2, levels, 2, early_rows, LANES)] * 2
        + [vmem(levels, 2, early_rows, LANES, dtype=jnp.int32), pltpu.SemaphoreType.DMA((12,))],
        (10000000, grid_bytes),
        {5: 7, 6: 8},
    )(c0, east_faces, north_faces, land_mask, vert_mix, sent_again, rows_b)
    got_b, got_rows_b = swap(sent_again, "lon_b"), swap(rows_b, "lat_b")
    c1, packed, own, terms, wet, mixing, _, row_own = call(
        inner_kernel,
        [ON_CHIP] * 4 + [SCALARS] + [ON_CHIP] * 7,
        shared + [vmem(8 * levels, wide)],
        [ON_CHIP] * 8,
        [],
        (40000000, 4 * grid_bytes),
        {5 + j: j for j in range(7)},
    )(c0, *near, vert_mix, *state_so_far)
    c1, next_side, next_again, next_rows_a, next_rows_b, correction = call(
        edge_kernel,
        [ON_CHIP] * 11,
        [state, side, side, rows2, rows2, side],
        [ON_CHIP] * 6,
        [],
        (1000000, 1000000),
        {10: 0},
    )(got_a, got_b, sent, got_rows_a, got_rows_b, own, row_own, packed, index, c0, c1)
    kept = [grid, vmem(TRACERS, levels, 2, tall + PAD, LANES), grid, grid, grid]
    c1, sent_side, sent_side_again, next_rows_a, next_rows_b, *kept_so_far = call(
        second_early_kernel,
        [ON_CHIP] * 9,
        [state, side, side, rows2, rows2] + kept,
        [ON_CHIP] * 10,
        [],
        (10000000, grid_bytes),
        {j: j for j in range(5)},
    )(c1, next_side, next_again, next_rows_a, next_rows_b, correction, terms, wet, mixing)
    new_a, new_b = swap(sent_side, "lon_a"), swap(sent_side_again, "lon_b")
    new_rows_a, new_rows_b = swap(next_rows_a, "lat_a"), swap(next_rows_b, "lat_b")
    c1, c2, *_ = call(
        second_kernel,
        [ON_CHIP] * 10,
        [state] + kept,
        [ON_CHIP] * 6,
        [],
        (40000000, 4 * grid_bytes),
        {j: j for j in range(6)},
    )(c1, *kept_so_far, correction, terms, wet, mixing)
    fields, density, _ = call(
        last_kernel,
        [ON_CHIP] * 15,
        [
            jax.ShapeDtypeStruct(tracers.shape, F32),
            jax.ShapeDtypeStruct(land_mask.shape, F32),
            vmem(TRACERS, levels, 2, tall, LANES),
        ],
        [ANYWHERE, ANYWHERE, ON_CHIP],
        [vmem(TRACERS, levels, 2, tall, LANES), level, pltpu.SemaphoreType.DMA((12,))],
        (4000000, 2 * grid_bytes),
        {14: 2},
    )(
        new_a, new_b, sent_side, got_a, got_b, new_rows_a, new_rows_b, got_rows_a, got_rows_b,
        own, row_own, index, c1, wet, c2,
    )
    return fields, density


def solution(mesh):
    in_specs = (
        P(None, None, "lat", "lon"),
        P(None, None, "lat", "lon"),
        P(None, None, "lat", "lon"),
        P(None, "lat", "lon"),
        P("lon"),
        P(),
    )
    out_specs = (P(None, None, "lat", "lon"), P(None, "lat", "lon"))
    pairs = pairings(mesh.shape["lat"], mesh.shape["lon"])

    def body(*args):
        return on_device(pairs, *args)

    return jax.shard_map(body, mesh=mesh, in_specs=in_specs, out_specs=out_specs, check_vma=False)
```
